128 devices in a mesh: gx: 8 (over z, y_hi), gy: 16 (over x, y_lo, core).
Axes of the slice: x: 4, y: 4 (y_hi: 2, y_lo: 2; y = y_hi * 2 + y_lo), z: 4, core: 2. Of those that a mesh axis runs over, the one named last changes fastest.
Arguments:
- les_wind: float32 [2, 8, 256, 1024], P(None, None, ('gx', 'gy')), may hold values from -0.4 to 0.4
- les_temp: float32 [8, 256, 1024], P(None, ('gx', 'gy')), may hold values from 0.8 to 1.25
- acoustic_start: float32 [3, 8, 512, 2048], P(None, None, 'gx', 'gy'), may hold values from -6 to 6
Outputs:
- acoustic_end: float32 [3, 8, 512, 2048], P(None, None, 'gx', 'gy')
The draws below stay inside these ranges and needn't reach their ends.
All inputs are finite; a program needn't handle non-finite values.
Results may differ from the reference program's by a relative error of at most 0.00013.
Values sent between devices are 32-bit elements; how exact they have to be, the bound alone decides.
No kernel may reach another device: no remote copies, remote signals or barrier semaphores. Data moves between devices by JAX's collectives and lax.ppermute only.
A program may use at most 128 MiB of HBM per device.

```python
import jax
import jax.numpy as jnp

L = 8
STEPS = 3
NX = 512
NY = 2048
CNX = 256
CNY = 1024


def steps_of(key, extent, shards, least, high):
    loudness = 1.0
    for position, parts in shards:
        heights = jax.random.uniform(jax.random.fold_in(jax.random.fold_in(key, 6), position), (parts,), jnp.float32, least / len(shards), high / len(shards))
        loudness = loudness * jnp.repeat(jnp.exp(heights), extent[position] // parts).reshape((-1,) + (1,) * (len(extent) - 1 - position))
    return loudness


def gaussian(key, dims, spread, limit, pieces=(), dtype=jnp.bfloat16):
    entries = spread * jax.random.normal(key, dims, jnp.float32)
    if pieces:
        entries = entries * steps_of(key, dims, pieces, -0.22, 0.18)
    return jnp.clip(entries, -limit, limit).astype(dtype)


def setup_inputs(seed: int = 0) -> dict:
    key_of = jax.random.split(jax.random.key(seed), 4)
    return {
        "les_wind": gaussian(key_of[0], (2, L, CNX, CNY), 0.12, 0.4, ((2, 128),), jnp.float32),
        "les_temp": jnp.clip(0.8 + 0.45 * jax.random.uniform(key_of[1], (L, CNX, CNY), jnp.float32) ** steps_of(key_of[1], (L, CNX, CNY), ((1, 128),), -0.2, 0.2), 0.8, 1.25),
        "acoustic_start": gaussian(key_of[2], (3, L, NX, NY), 1.0, 6.0, ((2, 8), (3, 16)), jnp.float32),
    }


time_step = 0.4


def refine_rows(extended):
    centre = extended[:, :, 1:-1]
    previous = extended[:, :, :-2]
    following = extended[:, :, 2:]
    even_cells = 0.75 * centre + 0.25 * previous
    odd_cells = 0.75 * centre + 0.25 * following
    joined = jnp.stack((even_cells, odd_cells), axis=3)
    return joined.reshape(joined.shape[0], joined.shape[1], 2 * centre.shape[2], centre.shape[3])


def refine_cols(extended):
    centre = extended[:, :, :, 1:-1]
    previous = extended[:, :, :, :-2]
    following = extended[:, :, :, 2:]
    even_cells = 0.75 * centre + 0.25 * previous
    odd_cells = 0.75 * centre + 0.25 * following
    joined = jnp.stack((even_cells, odd_cells), axis=4)
    return joined.reshape(joined.shape[0], joined.shape[1], centre.shape[2], 2 * centre.shape[3])


def along_rows(values):
    return (values[:, :, 0:-4, 2:-2] - 8.0 * values[:, :, 1:-3, 2:-2] + 8.0 * values[:, :, 3:-1, 2:-2] - values[:, :, 4:, 2:-2]) / 12.0


def along_cols(values):
    return (values[:, :, 2:-2, 0:-4] - 8.0 * values[:, :, 2:-2, 1:-3] + 8.0 * values[:, :, 2:-2, 3:-1] - values[:, :, 2:-2, 4:]) / 12.0


def tendency(extended, background):
    deriv_x = along_rows(extended)
    deriv_y = along_cols(extended)
    advect = background[0] * deriv_x + background[1] * deriv_y
    rate_pressure = -advect[0] - (deriv_x[1] + deriv_y[2])
    rate_east = -advect[1] - background[2] * deriv_x[0]
    rate_north = -advect[2] - background[2] * deriv_y[0]
    return jnp.stack((rate_pressure, rate_east, rate_north))


def wrapped(values):
    return jnp.pad(values, ((0, 0), (0, 0), (2, 2), (2, 2)), mode="wrap")


def one_level(coarse, acoustic):
    refined = refine_rows(jnp.pad(coarse, ((0, 0), (0, 0), (1, 1), (0, 0)), mode="wrap"))
    background = refine_cols(jnp.pad(refined, ((0, 0), (0, 0), (0, 0), (1, 1)), mode="wrap"))
    for repeat in range(STEPS):
        first = acoustic + time_step * tendency(wrapped(acoustic), background)
        second = 0.75 * acoustic + 0.25 * (first + time_step * tendency(wrapped(first), background))
        acoustic = (1.0 / 3.0) * acoustic + (2.0 / 3.0) * (second + time_step * tendency(wrapped(second), background))
    return acoustic


def reference(les_wind, les_temp, acoustic_start):
    coarse = jnp.concatenate((les_wind, les_temp[None]), axis=0)
    results = []
    for level in range(L):
        results.append(one_level(coarse[:, level:level + 1], acoustic_start[:, level:level + 1]))
    return jnp.concatenate(results, axis=1)
```

```python
import functools

import jax
import jax.numpy as jnp
import ml_dtypes
import numpy as np
from jax import lax
from jax.experimental import pallas as pl
from jax.experimental.pallas import tpu as pltpu
from jax.sharding import PartitionSpec as P

STEPS = 3
STAGES = 3 * STEPS
REACH = 2 * STAGES
LEVELS = 8
ROWS = 64
COLS = 128
EXT = ROWS + 2 * REACH
MARGIN = REACH // 2 + 1
CROWS = ROWS // 2
WINDOW = COLS // 2 + 2 * MARGIN
HALF = WINDOW // 2
RIGHT = 3 * REACH
RIM = 6 * REACH
EDGE = REACH // 3
MIDDLE = (ROWS - 2 * REACH) // 7
SIDE = EDGE + MIDDLE

time_step = 0.4
scale = time_step / 12.0

F32 = jnp.float32


def lanes():
    return lax.broadcasted_iota(jnp.int32, (LEVELS, COLS), 1)


def parity(axis):
    return lax.rem(lax.axis_index(axis), 2)


def swap_near(values, axis):
    return lax.ppermute(values, axis, [(i, i ^ 1) for i in range(lax.axis_size(axis))])


def swap_far(values, axis):
    count = lax.axis_size(axis)
    return lax.ppermute(
        values, axis, [(i, (i + 1) % count if i % 2 else (i - 1) % count) for i in range(count)]
    )


def roll(values, shift):
    if isinstance(shift, int):
        shift = shift % COLS
        if shift == 0:
            return values
    return pltpu.roll(values, shift, values.ndim - 1)


def slots():
    pieces = []
    for k in range(3):
        pieces.append((EDGE * k, EDGE, 0, k))
        pieces.append((ROWS - REACH + EDGE * k, EDGE, 0, 3 + k))
    for k in range(7):
        pieces.append((REACH + MIDDLE * k, MIDDLE, EDGE, k))
    return pieces


def coarse_pack_kernel(wind_ref, temp_ref, out_ref):
    lane = lanes()
    blocks = wind_ref.shape[-1] // COLS

    def windows(values):
        parts = [values[:, COLS * i : COLS * (i + 1)] for i in range(blocks)]
        near = [roll(part, MARGIN) for part in parts]
        far = [roll(part, COLS // 2 + MARGIN) for part in parts]
        result = []
        for i in range(blocks):
            result.append(jnp.where(lane < MARGIN, near[i - 1], near[i]))
            result.append(jnp.where(lane < COLS // 2 + MARGIN, far[i], far[(i + 1) % blocks]))
        return result

    for row in range(2):
        east = windows(wind_ref[0, :, row, :])
        north = windows(wind_ref[1, :, row, :])
        warm = windows(temp_ref[:, row, :])
        for j in range(2 * blocks):
            out_ref[j, row, 0] = jnp.where(lane < WINDOW, east[j], roll(warm[j], WINDOW))
            out_ref[j, row, 1] = jnp.where(lane < WINDOW, north[j], roll(warm[j], HALF))


def acoustic_pack_kernel(start_ref, tile_ref, x_near_ref, x_far_ref, y_near_ref, y_far_ref):
    x_odd, y_odd = parity("gx"), parity("gy")
    for f in range(3):
        for row in range(ROWS):
            tile_ref[f, row] = start_ref[pl.ds(f * LEVELS * ROWS + row, LEVELS, stride=ROWS), :]
    x_near_ref[...] = tile_ref[:, pl.ds((1 - x_odd) * (ROWS - REACH), REACH)]
    x_far_ref[...] = tile_ref[:, pl.ds(x_odd * (ROWS - REACH), REACH)]
    lane = lanes()
    for ref, first in (
        (y_near_ref, (1 - y_odd) * (COLS - REACH)),
        (y_far_ref, y_odd * (COLS - REACH)),
    ):
        for f in range(3):
            for group, size, base in ((0, EDGE, 0), (1, MIDDLE, EDGE)):
                packed = None
                for row, count, register, slot in slots():
                    if register != base:
                        continue
                    shift = lax.rem(REACH * slot - first + COLS, COLS)
                    moved = roll(tile_ref[f, row : row + count], shift)
                    if packed is None:
                        packed = moved
                    else:
                        inside = (lane >= REACH * slot) & (lane < REACH * (slot + 1))
                        packed = jnp.where(inside, moved, packed)
                ref[f, base : base + size] = packed


def second_pack_kernel(coarse_ref, y_near_ref, y_far_ref, x_near_ref, x_far_ref):
    x_odd, y_odd = parity("gx"), parity("gy")
    lane = lanes()
    width = 3 * REACH
    for ref, bottom in ((x_near_ref, 1 - x_odd), (x_far_ref, x_odd)):
        first = bottom * (CROWS - MARGIN)
        for i in range(MARGIN):
            for c in range(2):
                ref[2 * i + c] = coarse_ref[first + i, c]
        for f in range(3):
            for t in range(EDGE):
                start = bottom * width
                near = roll(y_near_ref[f, t], lax.rem((1 - y_odd) * width - start + COLS, COLS))
                far = roll(y_far_ref[f, t], lax.rem(y_odd * width - start + COLS, COLS))
                take_near = (lane >= width).astype(jnp.int32) == 1 - y_odd
                ref[2 * MARGIN + EDGE * f + t] = jnp.where(take_near, near, far)


def rim_of(main, left, right, lane):
    own = jnp.where(lane < RIGHT, roll(main, REACH), roll(main, RIGHT - (COLS - 2 * REACH)))
    own = jnp.where(lane < REACH, left, own)
    return jnp.where(lane >= RIM - REACH, right, own)


def step_rows(src, base, dst, background, c, r, count, stage):
    dx, dy, mid = [], [], []
    for f in range(3):
        block = src[c, f, pl.ds(r - 2, count + 4)]
        centre = block[2 : 2 + count]
        dx.append(8.0 * (block[3 : 3 + count] - block[1 : 1 + count]) - (block[4:] - block[:count]))
        dy.append(8.0 * (roll(centre, -1) - roll(centre, 1)) - (roll(centre, -2) - roll(centre, 2)))
        mid.append(centre)
    east = background[c, 0, pl.ds(r, count)]
    north = background[c, 1, pl.ds(r, count)]
    warm = background[c, 2, pl.ds(r, count)]
    change = (
        east * dx[0] + north * dy[0] + scale * (dx[1] + dy[2]),
        east * dx[1] + north * dy[1] + warm * dx[0],
        east * dx[2] + north * dy[2] + warm * dy[0],
    )
    for f in range(3):
        moved = mid[f] - change[f]
        if stage == 1:
            moved = 0.75 * base[c, f, pl.ds(r, count)] + 0.25 * moved
        elif stage == 2:
            moved = (1.0 / 3.0) * base[c, f, pl.ds(r, count)] + (2.0 / 3.0) * moved
        dst[c, f, pl.ds(r, count)] = moved


def solve_kernel(
    coarse_ref, tile_ref, y_near_ref, y_far_ref, x_near_ref, x_far_ref, s_near_ref, s_far_ref,
    east_table_ref, north_table_ref, out_ref, coarse, refined, background, state, first, second,
):
    x_odd, y_odd = parity("gx"), parity("gy")
    lane = lanes()
    coarse[MARGIN : MARGIN + CROWS] = coarse_ref[...]
    for ref, high in ((s_near_ref, 1 - x_odd), (s_far_ref, x_odd)):
        start = high * (MARGIN + CROWS)
        for i in range(MARGIN):
            for c in range(2):
                coarse[start + i, c] = ref[2 * i + c]

    @pl.loop(0, (CROWS + 2 * MARGIN) // 4)
    def _(step):
        m = step * 4
        products = []
        for c, table in ((0, east_table_ref), (1, north_table_ref)):
            values = coarse[pl.ds(m, 4), c].reshape(4 * LEVELS, COLS)
            high = values.astype(jnp.bfloat16)
            low = (values - high.astype(F32)).astype(jnp.bfloat16)
            both = jnp.concatenate((high, low), axis=1)
            products.append(jnp.dot(both, table[...], preferred_element_type=F32))
        warm = products[0][:, 2 * COLS :] + products[1][:, 2 * COLS :]
        for k in range(2):
            cut = slice(COLS * k, COLS * (k + 1))
            refined[k, 0, pl.ds(m, 4)] = products[0][:, cut].reshape(4, LEVELS, COLS)
            refined[k, 1, pl.ds(m, 4)] = products[1][:, cut].reshape(4, LEVELS, COLS)
            refined[k, 2, pl.ds(m, 4)] = warm[:, cut].reshape(4, LEVELS, COLS)

    @pl.loop(1, CROWS + 2 * MARGIN - 1)
    def _(m):
        for k in range(2):
            for f in range(3):
                block = refined[k, f, pl.ds(m - 1, 3)]
                centre = (0.75 * scale) * block[1]
                background[k, f, 2 * m - 2] = centre + (0.25 * scale) * block[0]
                background[k, f, 2 * m - 1] = centre + (0.25 * scale) * block[2]

    state[0, :, REACH : REACH + ROWS] = tile_ref[...]
    for row, count, register, slot in slots():
        take_near = (lane >= RIGHT).astype(jnp.int32) == 1 - y_odd
        for f in range(3):
            near = y_near_ref[f, register : register + count]
            far = y_far_ref[f, register : register + count]
            near = roll(near, lax.rem((1 - y_odd) * (RIM - REACH) - REACH * slot + COLS, COLS))
            far = roll(far, lax.rem(y_odd * (RIM - REACH) - REACH * slot + COLS, COLS))
            halo = jnp.where(take_near, near, far)
            main = tile_ref[f, row : row + count]
            state[1, f, REACH + row : REACH + row + count] = rim_of(main, halo, halo, lane)
    for main_ref, ref, high in ((x_near_ref, s_near_ref, 1 - x_odd), (x_far_ref, s_far_ref, x_odd)):
        start = high * (REACH + ROWS)
        state[0, :, pl.ds(start, REACH)] = main_ref[...]
        for f in range(3):
            corners = ref[2 * MARGIN + EDGE * f : 2 * MARGIN + EDGE * (f + 1)]
            for k in range(3):
                main = main_ref[f, EDGE * k : EDGE * (k + 1)]
                left = roll(corners, -REACH * k)
                right = roll(corners, RIM - REACH - RIGHT - REACH * k)
                state[1, f, pl.ds(start + EDGE * k, EDGE)] = rim_of(main, left, right, lane)

    buffers = (state, first, second, state)
    for step in range(STAGES):
        stage = step % 3
        low, top = 2 * (step + 1), EXT - 2 * (step + 1)

        @pl.loop(0, (top - low) // 4)
        def _(i):
            for c in range(2):
                step_rows(
                    buffers[stage], state, buffers[stage + 1], background, c, low + 4 * i, 4, stage
                )

    for f in range(3):

        @pl.loop(0, ROWS)
        def _(row):
            main = state[0, f, REACH + row]
            rim = state[1, f, REACH + row]
            value = jnp.where(lane < REACH, roll(rim, -REACH), main)
            value = jnp.where(lane >= COLS - REACH, roll(rim, COLS - 2 * REACH - RIGHT), value)
            out_ref[pl.ds(f * LEVELS * ROWS + row, LEVELS, stride=ROWS), :] = value


def tables():
    columns = np.full((2 * COLS,), -1000)
    columns[:COLS] = np.arange(COLS)
    columns[COLS : COLS + RIGHT] = np.arange(RIGHT) - REACH
    columns[COLS + RIGHT : COLS + RIM] = np.arange(RIGHT) + COLS - 2 * REACH
    window = np.zeros((WINDOW, 2 * COLS), np.float32)
    for j, column in enumerate(columns):
        if column > -1000:
            centre = column // 2 + MARGIN
            window[centre, j] = 0.75
            window[centre - 1 + 2 * (column % 2), j] = 0.25
    pair = []
    for part in (window[:HALF], window[HALF:]):
        table = np.zeros((COLS, 4 * COLS), np.float32)
        table[:WINDOW, : 2 * COLS] = window
        table[WINDOW : WINDOW + HALF, 2 * COLS :] = part
        pair.append(np.concatenate((table, table), axis=0).astype(ml_dtypes.bfloat16))
    return pair


def call(kernel, outputs, scratch=(), limit=48):
    return pl.pallas_call(
        kernel,
        out_shape=[jax.ShapeDtypeStruct(shape, F32) for shape in outputs],
        scratch_shapes=[pltpu.VMEM(shape, F32) for shape in scratch],
        compiler_params=pltpu.CompilerParams(vmem_limit_bytes=limit * 2**20),
    )


def local(les_wind, les_temp, acoustic_start):
    block = (LEVELS, COLS)
    groups = lax.axis_size("gy")
    (packed,) = call(coarse_pack_kernel, [(groups, 2, 2) + block])(les_wind, les_temp)
    coarse = lax.all_to_all(packed, "gy", split_axis=0, concat_axis=0, tiled=True)
    coarse = coarse.reshape((CROWS, 2) + block)
    tile, x_near, x_far, y_near, y_far = call(
        acoustic_pack_kernel,
        [(3, ROWS) + block] + 2 * [(3, REACH) + block] + 2 * [(3, SIDE) + block],
    )(acoustic_start.reshape(3 * LEVELS * ROWS, COLS))
    y_near, y_far = swap_near(y_near, "gy"), swap_far(y_far, "gy")
    x_near, x_far = swap_near(x_near, "gx"), swap_far(x_far, "gx")
    s_near, s_far = call(second_pack_kernel, 2 * [(2 * MARGIN + 3 * EDGE,) + block])(
        coarse, y_near, y_far
    )
    s_near, s_far = swap_near(s_near, "gx"), swap_far(s_far, "gx")
    east_table, north_table = tables()
    (end,) = call(
        solve_kernel,
        [(3 * LEVELS * ROWS, COLS)],
        scratch=[(CROWS + 2 * MARGIN, 2) + block, (2, 3, CROWS + 2 * MARGIN) + block]
        + 4 * [(2, 3, EXT) + block],
    )(
        coarse, tile, y_near, y_far, x_near, x_far, s_near, s_far,
        jnp.asarray(east_table), jnp.asarray(north_table),
    )
    return end.reshape(acoustic_start.shape)


def solution(mesh):
    in_specs = (
        P(None, None, ("gx", "gy"), None),
        P(None, ("gx", "gy"), None),
        P(None, None, "gx", "gy"),
    )
    out_specs = P(None, None, "gx", "gy")
    return jax.shard_map(local, mesh=mesh, in_specs=in_specs, out_specs=out_specs, check_vma=False)
```

```python
import jax
import jax.numpy as jnp
import ml_dtypes
import numpy as np
from jax import lax
from jax.experimental import pallas as pl
from jax.experimental.pallas import tpu as pltpu
from jax.sharding import PartitionSpec as P

STEPS = 3
STAGES = 3 * STEPS
REACH = 2 * STAGES
LEVELS = 8
ROWS = 64
COLS = 128
EXT = ROWS + 2 * REACH
MARGIN = REACH // 2 + 1
CROWS = ROWS // 2
WINDOW = COLS // 2 + 2 * MARGIN
HALF = WINDOW // 2
RIGHT = 3 * REACH
RIM = 6 * REACH
EDGE = REACH // 3
MIDDLE = (ROWS - 2 * REACH) // 7
HAND = 6
CHUNK = 16
SIDE = EDGE + MIDDLE

time_step = 0.4
scale = time_step / 12.0

F32 = jnp.float32


def lanes():
    return lax.broadcasted_iota(jnp.int32, (LEVELS, COLS), 1)


def parity(axis):
    return lax.rem(lax.axis_index(axis), 2)


def swap_near(values, axis):
    return lax.ppermute(values, axis, [(i, i ^ 1) for i in range(lax.axis_size(axis))])


def swap_far(values, axis):
    count = lax.axis_size(axis)
    return lax.ppermute(
        values, axis, [(i, (i + 1) % count if i % 2 else (i - 1) % count) for i in range(count)]
    )


def roll(values, shift):
    if isinstance(shift, int):
        shift = shift % COLS
        if shift == 0:
            return values
    return pltpu.roll(values, shift, values.ndim - 1)


def slots():
    pieces = []
    for k in range(3):
        pieces.append((EDGE * k, EDGE, 0, k))
        pieces.append((ROWS - REACH + EDGE * k, EDGE, 0, 3 + k))
    for k in range(7):
        pieces.append((REACH + MIDDLE * k, MIDDLE, EDGE, k))
    return pieces


def coarse_pack_kernel(wind_ref, temp_ref, out_ref):
    lane = lanes()
    blocks = wind_ref.shape[-1] // COLS

    def windows(values):
        parts = [values[:, COLS * i : COLS * (i + 1)] for i in range(blocks)]
        near = [roll(part, MARGIN) for part in parts]
        far = [roll(part, COLS // 2 + MARGIN) for part in parts]
        result = []
        for i in range(blocks):
            result.append(jnp.where(lane < MARGIN, near[i - 1], near[i]))
            result.append(jnp.where(lane < COLS // 2 + MARGIN, far[i], far[(i + 1) % blocks]))
        return result

    for row in range(2):
        east = windows(wind_ref[0, :, row, :])
        north = windows(wind_ref[1, :, row, :])
        warm = windows(temp_ref[:, row, :])
        for j in range(2 * blocks):
            out_ref[j, row, 0] = jnp.where(lane < WINDOW, east[j], roll(warm[j], WINDOW))
            out_ref[j, row, 1] = jnp.where(lane < WINDOW, north[j], roll(warm[j], HALF))


def acoustic_pack_kernel(start_ref, tile_ref, x_near_ref, x_far_ref, y_near_ref, y_far_ref):
    x_odd, y_odd = parity("gx"), parity("gy")
    for f in range(3):
        for row in range(ROWS):
            tile_ref[f, row] = start_ref[pl.ds(f * LEVELS * ROWS + row, LEVELS, stride=ROWS), :]
    x_near_ref[...] = tile_ref[:, pl.ds((1 - x_odd) * (ROWS - REACH), REACH)]
    x_far_ref[...] = tile_ref[:, pl.ds(x_odd * (ROWS - REACH), REACH)]
    lane = lanes()
    for ref, first in (
        (y_near_ref, (1 - y_odd) * (COLS - REACH)),
        (y_far_ref, y_odd * (COLS - REACH)),
    ):
        for f in range(3):
            for group, size, base in ((0, EDGE, 0), (1, MIDDLE, EDGE)):
                packed = None
                for row, count, register, slot in slots():
                    if register != base:
                        continue
                    shift = lax.rem(REACH * slot - first + COLS, COLS)
                    moved = roll(tile_ref[f, row : row + count], shift)
                    if packed is None:
                        packed = moved
                    else:
                        inside = (lane >= REACH * slot) & (lane < REACH * (slot + 1))
                        packed = jnp.where(inside, moved, packed)
                ref[f, base : base + size] = packed


def second_pack_kernel(coarse_ref, y_near_ref, y_far_ref, x_near_ref, x_far_ref):
    x_odd, y_odd = parity("gx"), parity("gy")
    lane = lanes()
    width = 3 * REACH
    for ref, bottom in ((x_near_ref, 1 - x_odd), (x_far_ref, x_odd)):
        first = bottom * (CROWS - MARGIN)
        for i in range(MARGIN):
            for c in range(2):
                ref[2 * i + c] = coarse_ref[first + i, c]
        for f in range(3):
            for t in range(EDGE):
                start = bottom * width
                near = roll(y_near_ref[f, t], lax.rem((1 - y_odd) * width - start + COLS, COLS))
                far = roll(y_far_ref[f, t], lax.rem(y_odd * width - start + COLS, COLS))
                take_near = (lane >= width).astype(jnp.int32) == 1 - y_odd
                ref[2 * MARGIN + EDGE * f + t] = jnp.where(take_near, near, far)


def rim_of(main, left, right, lane):
    own = jnp.where(lane < RIGHT, roll(main, REACH), roll(main, RIGHT - (COLS - 2 * REACH)))
    own = jnp.where(lane < REACH, left, own)
    return jnp.where(lane >= RIM - REACH, right, own)


def products(blocks, table_ref):
    counts = [block.shape[0] * LEVELS for block in blocks]
    values = jnp.concatenate(
        [block.reshape(count, COLS) for block, count in zip(blocks, counts)], axis=0
    )
    high = values.astype(jnp.bfloat16)
    low = (values - high.astype(F32)).astype(jnp.bfloat16)
    result = jnp.dot(
        jnp.concatenate((high, low), axis=1), table_ref[...], preferred_element_type=F32
    )
    pieces, start = [], 0
    for count in counts:
        pieces.append(result[start : start + count])
        start += count
    return pieces


def stage_blocks(jobs, stage, table_ref):
    centres = [[rows[2:-2] for rows in source] for source, _, _, _ in jobs]
    across = products([centre for job in centres for centre in job], table_ref)
    for index, (source, base, background, store) in enumerate(jobs):
        mid = centres[index]
        count = mid[0].shape[0]
        dy = [across[3 * index + f].reshape(mid[0].shape) for f in range(3)]
        dx = [
            8.0 * (rows[3 : 3 + count] - rows[1 : 1 + count]) - (rows[4:] - rows[:count])
            for rows in source
        ]
        east, north, warm = background
        change = (
            east * dx[0] + north * dy[0] + scale * (dx[1] + dy[2]),
            east * dx[1] + north * dy[1] + warm * dx[0],
            east * dx[2] + north * dy[2] + warm * dy[0],
        )
        for f in range(3):
            moved = mid[f] - change[f]
            if stage == 1:
                moved = 0.75 * base[f] + 0.25 * moved
            elif stage == 2:
                moved = (1.0 / 3.0) * base[f] + (2.0 / 3.0) * moved
            store(f, moved)


def refine_tables(values, east_table_ref, north_table_ref, store):
    n = values.shape[0]
    (first,) = products([values[:, 0]], east_table_ref)
    (second,) = products([values[:, 1]], north_table_ref)
    warm = first[:, 2 * COLS :] + second[:, 2 * COLS :]
    for k in range(2):
        cut = slice(COLS * k, COLS * (k + 1))
        for f, result in enumerate((first, second, warm)):
            store(k, f, result[:, cut].reshape(n, LEVELS, COLS))


def merged(main, rim, lane):
    value = jnp.where(lane < REACH, roll(rim, -REACH), main)
    return jnp.where(lane >= COLS - REACH, roll(rim, COLS - 2 * REACH - RIGHT), value)


def inner_kernel(
    coarse_ref, tile_ref, y_near_ref, y_far_ref, east_table_ref, north_table_ref, table_ref,
    edges_ref, inside_ref, refined_ref, background, state, first, second,
):
    y_odd = parity("gy")
    lane = lanes()

    def keep(k, f, start):
        def store(values):
            refined_ref[k, f, start : start + values.shape[0]] = values

        return store

    for start in range(0, CROWS, CHUNK):
        refine_tables(
            coarse_ref[start : start + CHUNK],
            east_table_ref,
            north_table_ref,
            lambda k, f, values, start=start: keep(k, f, start)(values),
        )
    for k in range(2):
        for f in range(3):
            refine_rows(refined_ref, k, f, 0, CROWS, background, 0)

    take_near = (lane >= RIGHT).astype(jnp.int32) == 1 - y_odd
    state[0] = tile_ref[...]
    for row, count, register, slot in slots():
        near_shift = lax.rem((1 - y_odd) * (RIM - REACH) - REACH * slot + COLS, COLS)
        far_shift = lax.rem(y_odd * (RIM - REACH) - REACH * slot + COLS, COLS)
        for f in range(3):
            near = roll(y_near_ref[f, register : register + count], near_shift)
            far = roll(y_far_ref[f, register : register + count], far_shift)
            halo = jnp.where(take_near, near, far)
            state[1, f, row : row + count] = rim_of(tile_ref[f, row : row + count], halo, halo, lane)

    buffers = (state, first, second, state)
    for s in range(STAGES):
        source, target = buffers[s % 3], buffers[s % 3 + 1]
        for c in range(2):
            for f in range(3):
                edges_ref[s, c, f, :HAND] = source[c, f, 2 * s : 2 * s + HAND]
                edges_ref[s, c, f, HAND:] = source[c, f, ROWS - 2 * s - HAND : ROWS - 2 * s]
        low, top = 2 * (s + 1), ROWS - 2 * (s + 1)
        for start in range(low, top, CHUNK):
            stop = min(start + CHUNK, top)
            jobs = []
            for c in range(2):

                def store(f, values, c=c):
                    target[c, f, start:stop] = values

                jobs.append((
                    [source[c, f, start - 2 : stop + 2] for f in range(3)],
                    [state[c, f, start:stop] for f in range(3)],
                    [background[c, f, start:stop] for f in range(3)],
                    store,
                ))
            stage_blocks(jobs, s % 3, table_ref)
    for f in range(3):
        rows = slice(REACH, ROWS - REACH)
        inside_ref[f] = merged(state[0, f, rows], state[1, f, rows], lane)


def refine_rows(refined, k, f, start, count, background, first):
    block = refined[k, f, start : start + count]
    centre = (0.75 * scale) * block
    side = (0.25 * scale) * block
    odd = centre[:-1] + side[1:]
    even = centre[1:] + side[:-1]
    for i in range(count - 1):
        background[k, f, first + 2 * i + 1] = odd[i]
        background[k, f, first + 2 * i + 2] = even[i]


def outer_kernel(
    x_near_ref, x_far_ref, s_near_ref, s_far_ref, edges_ref, inside_ref, refined_ref,
    east_table_ref, north_table_ref, table_ref, out_ref, coarse, refined, background, state, first, second,
):
    x_odd = parity("gx")
    lane = lanes()
    for ref, high in ((s_near_ref, 1 - x_odd), (s_far_ref, x_odd)):
        for i in range(MARGIN):
            for c in range(2):
                coarse[high * MARGIN + i, c] = ref[2 * i + c]

    def store(k, f, values):
        refined[k, f, 0:MARGIN] = values[:MARGIN]
        refined[k, f, MARGIN : 2 * MARGIN] = refined_ref[k, f, 0:MARGIN]
        refined[k, f, 2 * MARGIN : 3 * MARGIN] = refined_ref[k, f, CROWS - MARGIN : CROWS]
        refined[k, f, 3 * MARGIN : 4 * MARGIN] = values[MARGIN:]

    refine_tables(coarse[...], east_table_ref, north_table_ref, store)
    for side in range(2):
        for k in range(2):
            for f in range(3):
                refine_rows(refined, k, f, 2 * MARGIN * side, 2 * MARGIN, background.at[side], 0)

    for main_ref, ref, high in ((x_near_ref, s_near_ref, 1 - x_odd), (x_far_ref, s_far_ref, x_odd)):
        for f in range(3):
            corners = ref[2 * MARGIN + EDGE * f : 2 * MARGIN + EDGE * (f + 1)]
            for k in range(3):
                main = main_ref[f, EDGE * k : EDGE * (k + 1)]
                left = roll(corners, -REACH * k)
                right = roll(corners, RIM - REACH - RIGHT - REACH * k)
                start = high * REACH + EDGE * k
                state[high, 0, f, pl.ds(start, EDGE)] = main
                state[high, 1, f, pl.ds(start, EDGE)] = rim_of(main, left, right, lane)

    buffers = (state, first, second, state)
    for s in range(STAGES):
        source, target = buffers[s % 3], buffers[s % 3 + 1]
        origin = s - s % 3
        jobs = []
        for side in range(2):
            for c in range(2):
                if side == 0:
                    low = 2 * (s + 1)
                    rows = [
                        jnp.concatenate((source[0, c, f, low - 2 : REACH + 2 * s], edges_ref[s, c, f, :4]))
                        for f in range(3)
                    ]
                    base = [
                        jnp.concatenate((
                            state[0, c, f, low : REACH + 2 * origin],
                            edges_ref[origin, c, f, : low - 2 * origin],
                        ))
                        for f in range(3)
                    ]
                else:
                    low = REACH - 2 * (s + 1)
                    rows = [
                        jnp.concatenate((
                            edges_ref[s, c, f, 2 * HAND - 4 :],
                            source[1, c, f, REACH - 2 * s : 2 * REACH - 2 * s],
                        ))
                        for f in range(3)
                    ]
                    base = [
                        jnp.concatenate((
                            edges_ref[origin, c, f, 2 * HAND - (REACH - 2 * origin - low) :],
                            state[1, c, f, REACH - 2 * origin : low + REACH],
                        ))
                        for f in range(3)
                    ]

                def store(f, values, side=side, c=c, low=low):
                    target[side, c, f, low : low + REACH] = values

                near = [background[side, c, f, low + 2 : low + 2 + REACH] for f in range(3)]
                jobs.append((rows, base, near, store))
        stage_blocks(jobs, s % 3, table_ref)

    for f in range(3):
        for side, start in ((0, 0), (1, ROWS - REACH)):
            rows = slice(REACH * (1 - side), REACH * (1 - side) + REACH)
            values = merged(state[side, 0, f, rows], state[side, 1, f, rows], lane)
            for row in range(REACH):
                out_ref[pl.ds(f * LEVELS * ROWS + start + row, LEVELS, stride=ROWS), :] = values[row]
        for row in range(ROWS - 2 * REACH):
            at = f * LEVELS * ROWS + REACH + row
            out_ref[pl.ds(at, LEVELS, stride=ROWS), :] = inside_ref[f, row]


def difference_table():
    table = np.zeros((COLS, COLS), np.float32)
    for j in range(COLS):
        for offset, weight in ((1, 8.0), (-1, -8.0), (2, -1.0), (-2, 1.0)):
            table[(j + offset) % COLS, j] = weight
    return np.concatenate((table, table), axis=0).astype(ml_dtypes.bfloat16)


def tables():
    columns = np.full((2 * COLS,), -1000)
    columns[:COLS] = np.arange(COLS)
    columns[COLS : COLS + RIGHT] = np.arange(RIGHT) - REACH
    columns[COLS + RIGHT : COLS + RIM] = np.arange(RIGHT) + COLS - 2 * REACH
    window = np.zeros((WINDOW, 2 * COLS), np.float32)
    for j, column in enumerate(columns):
        if column > -1000:
            centre = column // 2 + MARGIN
            window[centre, j] = 0.75
            window[centre - 1 + 2 * (column % 2), j] = 0.25
    pair = []
    for part in (window[:HALF], window[HALF:]):
        table = np.zeros((COLS, 4 * COLS), np.float32)
        table[:WINDOW, : 2 * COLS] = window
        table[WINDOW : WINDOW + HALF, 2 * COLS :] = part
        pair.append(np.concatenate((table, table), axis=0).astype(ml_dtypes.bfloat16))
    return pair


def call(kernel, outputs, scratch=(), limit=48, microseconds=1):
    return pl.pallas_call(
        kernel,
        out_shape=[jax.ShapeDtypeStruct(shape, F32) for shape in outputs],
        scratch_shapes=[pltpu.VMEM(shape, F32) for shape in scratch],
        compiler_params=pltpu.CompilerParams(vmem_limit_bytes=limit * 2**20),
        cost_estimate=pl.CostEstimate(
            flops=0, bytes_accessed=3_000_000 * microseconds, transcendentals=0
        ),
    )


def local(les_wind, les_temp, acoustic_start):
    block = (LEVELS, COLS)
    groups = lax.axis_size("gy")
    (packed,) = call(coarse_pack_kernel, [(groups, 2, 2) + block])(les_wind, les_temp)
    coarse = lax.all_to_all(packed, "gy", split_axis=0, concat_axis=0, tiled=True)
    coarse = coarse.reshape((CROWS, 2) + block)
    tile, x_near, x_far, y_near, y_far = call(
        acoustic_pack_kernel,
        [(3, ROWS) + block] + 2 * [(3, REACH) + block] + 2 * [(3, SIDE) + block],
    )(acoustic_start.reshape(3 * LEVELS * ROWS, COLS))
    y_near, y_far = swap_near(y_near, "gy"), swap_far(y_far, "gy")
    x_near, x_far = swap_near(x_near, "gx"), swap_far(x_far, "gx")
    s_near, s_far = call(second_pack_kernel, 2 * [(2 * MARGIN + 3 * EDGE,) + block])(
        coarse, y_near, y_far
    )
    s_near, s_far = swap_near(s_near, "gx"), swap_far(s_far, "gx")
    east_table, north_table = (jnp.asarray(table) for table in tables())
    table = jnp.asarray(difference_table())
    edges, inside, refined = call(
        inner_kernel,
        [(STAGES, 2, 3, 2 * HAND) + block, (3, ROWS - 2 * REACH) + block, (2, 3, CROWS) + block],
        scratch=4 * [(2, 3, ROWS) + block],
        microseconds=6,
    )(coarse, tile, y_near, y_far, east_table, north_table, table)
    (end,) = call(
        outer_kernel,
        [(3 * LEVELS * ROWS, COLS)],
        scratch=[(2 * MARGIN, 2) + block, (2, 3, 4 * MARGIN) + block, (2, 2, 3, 4 * MARGIN) + block]
        + 3 * [(2, 2, 3, 2 * REACH) + block],
        microseconds=6,
    )(x_near, x_far, s_near, s_far, edges, inside, refined, east_table, north_table, table)
    return end.reshape(acoustic_start.shape)


def solution(mesh):
    in_specs = (
        P(None, None, ("gx", "gy"), None),
        P(None, ("gx", "gy"), None),
        P(None, None, "gx", "gy"),
    )
    out_specs = P(None, None, "gx", "gy")
    return jax.shard_map(local, mesh=mesh, in_specs=in_specs, out_specs=out_specs, check_vma=False)
```

```python
import jax
import jax.numpy as jnp
import ml_dtypes
import numpy as np
from jax import lax
from jax.experimental import pallas as pl
from jax.experimental.pallas import tpu as pltpu
from jax.sharding import PartitionSpec as P

STEPS = 3
STAGES = 3 * STEPS
REACH = 2 * STAGES
LEVELS = 8
ROWS = 64
COLS = 128
EXT = ROWS + 2 * REACH
MARGIN = REACH // 2 + 1
CROWS = ROWS // 2
WINDOW = COLS // 2 + 2 * MARGIN
HALF = WINDOW // 2
RIGHT = 3 * REACH
RIM = 6 * REACH
EDGE = REACH // 3
MIDDLE = (ROWS - 2 * REACH) // 7
HROWS = REACH // 2
PAIRS = REACH // 2
PER = COLS // REACH
CREGS = -(-2 * PAIRS // PER)
HAND = 6
CHUNK = 16
PACK_LIMIT = 60
SIDE = EDGE + MIDDLE

time_step = 0.4
scale = time_step / 12.0

F32 = jnp.float32


def lanes():
    return lax.broadcasted_iota(jnp.int32, (LEVELS, COLS), 1)


def parity(axis):
    return lax.rem(lax.axis_index(axis), 2)


def swap_near(values, axis):
    return lax.ppermute(values, axis, [(i, i ^ 1) for i in range(lax.axis_size(axis))])


def swap_far(values, axis):
    count = lax.axis_size(axis)
    return lax.ppermute(
        values, axis, [(i, (i + 1) % count if i % 2 else (i - 1) % count) for i in range(count)]
    )


def roll(values, shift):
    if isinstance(shift, int):
        shift = shift % COLS
        if shift == 0:
            return values
    return pltpu.roll(values, shift, values.ndim - 1)


def slots():
    pieces = []
    for k in range(3):
        pieces.append((EDGE * k, EDGE, 0, k))
        pieces.append((ROWS - REACH + EDGE * k, EDGE, 0, 3 + k))
    for k in range(7):
        pieces.append((REACH + MIDDLE * k, MIDDLE, EDGE, k))
    return pieces


def pack_coarse(wind_ref, temp_ref, out_ref):
    lane = lanes()
    blocks = wind_ref.shape[-1] // COLS

    def windows(values):
        parts = [values[:, COLS * i : COLS * (i + 1)] for i in range(blocks)]
        near = [roll(part, MARGIN) for part in parts]
        far = [roll(part, COLS // 2 + MARGIN) for part in parts]
        result = []
        for i in range(blocks):
            result.append(jnp.where(lane < MARGIN, near[i - 1], near[i]))
            result.append(jnp.where(lane < COLS // 2 + MARGIN, far[i], far[(i + 1) % blocks]))
        return result

    for row in range(2):
        east = windows(wind_ref[0, :, row, :])
        north = windows(wind_ref[1, :, row, :])
        warm = windows(temp_ref[:, row, :])
        for j in range(2 * blocks):
            out_ref[j, row, 0] = jnp.where(lane < WINDOW, east[j], roll(warm[j], WINDOW))
            out_ref[j, row, 1] = jnp.where(lane < WINDOW, north[j], roll(warm[j], HALF))


def pack_kernel(
    wind_hbm, temp_hbm, start_hbm, out_ref, tile_ref, x_near_ref, x_far_ref, y_near_ref, y_far_ref,
    wind_ref, temp_ref, start_ref, sems,
):
    x_odd, y_odd = parity("gx"), parity("gy")
    wind_copy = pltpu.make_async_copy(wind_hbm, wind_ref, sems.at[0])
    temp_copy = pltpu.make_async_copy(temp_hbm, temp_ref, sems.at[1])
    start_copy = pltpu.make_async_copy(start_hbm, start_ref, sems.at[2])
    wind_copy.start()
    temp_copy.start()
    start_copy.start()
    wind_copy.wait()
    temp_copy.wait()
    pack_coarse(wind_ref, temp_ref, out_ref)
    start_copy.wait()
    for f in range(3):
        for row in range(ROWS):
            tile_ref[f, row] = start_ref[pl.ds(f * LEVELS * ROWS + row, LEVELS, stride=ROWS), :]
    x_near_ref[...] = tile_ref[:, pl.ds((1 - x_odd) * (ROWS - REACH), REACH)]
    x_far_ref[...] = tile_ref[:, pl.ds(x_odd * (ROWS - REACH), REACH)]
    lane = lanes()
    for ref, first in (
        (y_near_ref, (1 - y_odd) * (COLS - REACH)),
        (y_far_ref, y_odd * (COLS - REACH)),
    ):
        for f in range(3):
            for size, base in ((EDGE, 0), (MIDDLE, EDGE)):
                packed = None
                for row, count, register, slot in slots():
                    if register != base:
                        continue
                    shift = lax.rem(REACH * slot - first + COLS, COLS)
                    moved = roll(tile_ref[f, row : row + count], shift)
                    if packed is None:
                        packed = moved
                    else:
                        inside = (lane >= REACH * slot) & (lane < REACH * (slot + 1))
                        packed = jnp.where(inside, moved, packed)
                ref[f, base : base + size] = packed


def corner_slot(away, right):
    pair = min(away, REACH - 2 - away)
    register, slot = divmod(pair + PAIRS * right, PER)
    offset = 0
    if away > pair:
        offset = (REACH - 1 - pair) * (1 if right else -1)
    return register, REACH * slot, offset


def corner_lanes(away, right, lane):
    _, first, _ = corner_slot(away, right)
    pair = min(away, REACH - 2 - away)
    if away == pair:
        low, high = (0, REACH - 1 - away) if right else (1 + away, REACH)
    else:
        low, high = (REACH - 1 - pair, REACH) if right else (0, pair + 1)
    return (lane >= first + low) & (lane < first + high)


def second_pack_kernel(coarse_ref, y_near_ref, y_far_ref, x_near_ref, x_far_ref):
    x_odd, y_odd = parity("gx"), parity("gy")
    lane = lanes()
    for ref, bottom in ((x_near_ref, 1 - x_odd), (x_far_ref, x_odd)):
        first = bottom * (CROWS - HROWS)
        for i in range(HROWS):
            for c in range(2):
                ref[2 * i + c] = coarse_ref[first + i, c]
        for f in range(3):
            packed = [None] * CREGS
            for away in range(REACH - 1):
                slot, t = divmod(away, EDGE)
                register = t + bottom * (EDGE - 1 - 2 * t)
                source = REACH * (slot + bottom * (5 - 2 * slot))
                for right in range(2):
                    target, start, offset = corner_slot(away, right)
                    take_far = y_odd if right else 1 - y_odd
                    near = y_near_ref[f, register]
                    far = y_far_ref[f, register]
                    halo = jnp.where(jnp.full_like(lane, take_far) == 1, far, near)
                    moved = roll(halo, lax.rem(start + offset - source + 3 * COLS, COLS))
                    if packed[target] is None:
                        packed[target] = moved
                    else:
                        inside = corner_lanes(away, right, lane)
                        packed[target] = jnp.where(inside, moved, packed[target])
            for target in range(CREGS):
                ref[2 * HROWS + CREGS * f + target] = packed[target]


def rim_of(main, left, right, lane):
    own = jnp.where(lane < RIGHT, roll(main, REACH), roll(main, RIGHT - (COLS - 2 * REACH)))
    own = jnp.where(lane < REACH, left, own)
    return jnp.where(lane >= RIM - REACH, right, own)


def products(blocks, table_ref):
    counts = [block.shape[0] * LEVELS for block in blocks]
    values = jnp.concatenate(
        [block.reshape(count, COLS) for block, count in zip(blocks, counts)], axis=0
    )
    high = values.astype(jnp.bfloat16)
    low = (values - high.astype(F32)).astype(jnp.bfloat16)
    result = jnp.dot(
        jnp.concatenate((high, low), axis=1), table_ref[...], preferred_element_type=F32
    )
    pieces, start = [], 0
    for count in counts:
        pieces.append(result[start : start + count])
        start += count
    return pieces


def stage_products(jobs, table_ref):
    return products([rows[2:-2] for source, _, _, _ in jobs for rows in source], table_ref)


def stage_sums(jobs, across, stage):
    for index, (source, base, background, store) in enumerate(jobs):
        mid = [rows[2:-2] for rows in source]
        count = mid[0].shape[0]
        dy = [across[3 * index + f].reshape(mid[0].shape) for f in range(3)]
        dx = [
            8.0 * (rows[3 : 3 + count] - rows[1 : 1 + count]) - (rows[4:] - rows[:count])
            for rows in source
        ]
        east, north, warm = background
        change = (
            east * dx[0] + north * dy[0] + scale * (dx[1] + dy[2]),
            east * dx[1] + north * dy[1] + warm * dx[0],
            east * dx[2] + north * dy[2] + warm * dy[0],
        )
        for f in range(3):
            moved = mid[f] - change[f]
            if stage == 1:
                moved = 0.75 * base[f] + 0.25 * moved
            elif stage == 2:
                moved = (1.0 / 3.0) * base[f] + (2.0 / 3.0) * moved
            store(f, moved)


def refine_tables(values, east_table_ref, north_table_ref, store):
    n = values.shape[0]
    (first,) = products([values[:, 0]], east_table_ref)
    (second,) = products([values[:, 1]], north_table_ref)
    warm = first[:, 2 * COLS :] + second[:, 2 * COLS :]
    for k in range(2):
        cut = slice(COLS * k, COLS * (k + 1))
        for f, result in enumerate((first, second, warm)):
            store(k, f, result[:, cut].reshape(n, LEVELS, COLS))


def merged(main, rim, lane):
    value = jnp.where(lane < REACH, roll(rim, -REACH), main)
    return jnp.where(lane >= COLS - REACH, roll(rim, COLS - 2 * REACH - RIGHT), value)


def inner_kernel(
    coarse_ref, tile_ref, y_near_ref, y_far_ref, east_table_ref, north_table_ref, table_ref,
    edges_ref, inside_ref, refined_ref, background, state, first, second,
):
    y_odd = parity("gy")
    lane = lanes()

    def keep(k, f, start):
        def store(values):
            refined_ref[k, f, start : start + values.shape[0]] = values

        return store

    for start in range(0, CROWS, CHUNK):
        refine_tables(
            coarse_ref[start : start + CHUNK],
            east_table_ref,
            north_table_ref,
            lambda k, f, values, start=start: keep(k, f, start)(values),
        )
    for k in range(2):
        for f in range(3):
            refine_rows(refined_ref, k, f, 0, CROWS, background, 0)

    take_near = (lane >= RIGHT).astype(jnp.int32) == 1 - y_odd
    state[0] = tile_ref[...]
    for row, count, register, slot in slots():
        near_shift = lax.rem((1 - y_odd) * (RIM - REACH) - REACH * slot + COLS, COLS)
        far_shift = lax.rem(y_odd * (RIM - REACH) - REACH * slot + COLS, COLS)
        for f in range(3):
            near = roll(y_near_ref[f, register : register + count], near_shift)
            far = roll(y_far_ref[f, register : register + count], far_shift)
            halo = jnp.where(take_near, near, far)
            state[1, f, row : row + count] = rim_of(tile_ref[f, row : row + count], halo, halo, lane)

    buffers = (state, first, second, state)
    for s in range(STAGES):
        source, target = buffers[s % 3], buffers[s % 3 + 1]
        for c in range(2):
            for f in range(3):
                edges_ref[s, c, f, :HAND] = source[c, f, 2 * s : 2 * s + HAND]
                edges_ref[s, c, f, HAND:] = source[c, f, ROWS - 2 * s - HAND : ROWS - 2 * s]
        low, top = 2 * (s + 1), ROWS - 2 * (s + 1)
        for start in range(low, top, CHUNK):
            stop = min(start + CHUNK, top)
            jobs = []
            for c in range(2):

                def store(f, values, c=c):
                    target[c, f, start:stop] = values

                jobs.append((
                    [source[c, f, start - 2 : stop + 2] for f in range(3)],
                    [state[c, f, start:stop] for f in range(3)],
                    [background[c, f, start:stop] for f in range(3)],
                    store,
                ))
            stage_sums(jobs, stage_products(jobs, table_ref), s % 3)
    for f in range(3):
        rows = slice(REACH, ROWS - REACH)
        inside_ref[f] = merged(state[0, f, rows], state[1, f, rows], lane)


def refine_rows(refined, k, f, start, count, background, first):
    block = refined[k, f, start : start + count]
    centre = (0.75 * scale) * block
    side = (0.25 * scale) * block
    odd = centre[:-1] + side[1:]
    even = centre[1:] + side[:-1]
    for i in range(count - 1):
        background[k, f, first + 2 * i + 1] = odd[i]
        background[k, f, first + 2 * i + 2] = even[i]


def outer_kernel(
    x_near_ref, x_far_ref, s_near_ref, s_far_ref, edges_ref, inside_ref, refined_ref,
    east_table_ref, north_table_ref, table_ref, out_ref, refined, background, state, first, second,
):
    x_odd = parity("gx")
    lane = lanes()
    own = MARGIN + HROWS
    for k in range(2):
        for f in range(3):
            refined[k, f, HROWS:own] = refined_ref[k, f, 0:MARGIN]
            refined[k, f, own : own + MARGIN] = refined_ref[k, f, CROWS - MARGIN : CROWS]
    for ref, high in ((s_near_ref, 1 - x_odd), (s_far_ref, x_odd)):

        def store(k, f, values, high=high):
            refined[k, f, pl.ds(high * (own + MARGIN), HROWS)] = values

        values = ref[: 2 * HROWS].reshape(HROWS, 2, LEVELS, COLS)
        refine_tables(values, east_table_ref, north_table_ref, store)
    for side in range(2):
        for k in range(2):
            for f in range(3):
                refine_rows(refined, k, f, own * side, own, background.at[side], 0)

    for main_ref, ref, high in ((x_near_ref, s_near_ref, 1 - x_odd), (x_far_ref, s_far_ref, x_odd)):
        for f in range(3):
            state[high, 0, f, pl.ds(high * REACH, REACH)] = main_ref[f]
            for away in range(REACH):
                row = REACH - 1 - away + high * (2 * away - REACH + 1)
                main = main_ref[f, row]
                halo = []
                for right in range(2):
                    register, start, offset = corner_slot(min(away, REACH - 2), right)
                    values = ref[2 * HROWS + CREGS * f + register]
                    halo.append(roll(values, (RIM - REACH) * right - start - offset))
                state[high, 1, f, high * REACH + row] = rim_of(main, halo[0], halo[1], lane)

    buffers = (state, first, second, state)

    def jobs_of(side, s):
        source, target = buffers[s % 3], buffers[s % 3 + 1]
        origin = s - s % 3
        jobs = []
        for c in range(2):
            if side == 0:
                low = 2 * (s + 1)
                rows = [
                    jnp.concatenate((source[0, c, f, low - 2 : REACH + 2 * s], edges_ref[s, c, f, :4]))
                    for f in range(3)
                ]
                base = [
                    jnp.concatenate((
                        state[0, c, f, low : REACH + 2 * origin],
                        edges_ref[origin, c, f, : low - 2 * origin],
                    ))
                    for f in range(3)
                ]
            else:
                low = REACH - 2 * (s + 1)
                rows = [
                    jnp.concatenate((
                        edges_ref[s, c, f, 2 * HAND - 4 :],
                        source[1, c, f, REACH - 2 * s : 2 * REACH - 2 * s],
                    ))
                    for f in range(3)
                ]
                base = [
                    jnp.concatenate((
                        edges_ref[origin, c, f, 2 * HAND - (REACH - 2 * origin - low) :],
                        state[1, c, f, REACH - 2 * origin : low + REACH],
                    ))
                    for f in range(3)
                ]

            def store(f, values, c=c):
                target[side, c, f, low : low + REACH] = values

            start = low + 2 * side
            near = [background[side, c, f, start : start + REACH] for f in range(3)]
            jobs.append((rows, base, near, store))
        return jobs

    waiting = [None, None]
    for s in range(STAGES + 1):
        for side in range(2):
            if waiting[side] is not None:
                stage_sums(waiting[side][0], waiting[side][1], (s - 1) % 3)
            if s < STAGES:
                jobs = jobs_of(side, s)
                waiting[side] = (jobs, stage_products(jobs, table_ref))

    for f in range(3):
        for side, start in ((0, 0), (1, ROWS - REACH)):
            rows = slice(REACH * (1 - side), REACH * (1 - side) + REACH)
            values = merged(state[side, 0, f, rows], state[side, 1, f, rows], lane)
            for row in range(REACH):
                out_ref[pl.ds(f * LEVELS * ROWS + start + row, LEVELS, stride=ROWS), :] = values[row]
        for row in range(ROWS - 2 * REACH):
            at = f * LEVELS * ROWS + REACH + row
            out_ref[pl.ds(at, LEVELS, stride=ROWS), :] = inside_ref[f, row]


def difference_table():
    table = np.zeros((COLS, COLS), np.float32)
    for j in range(COLS):
        for offset, weight in ((1, 8.0), (-1, -8.0), (2, -1.0), (-2, 1.0)):
            table[(j + offset) % COLS, j] = weight
    return np.concatenate((table, table), axis=0).astype(ml_dtypes.bfloat16)


def tables():
    columns = np.full((2 * COLS,), -1000)
    columns[:COLS] = np.arange(COLS)
    columns[COLS : COLS + RIGHT] = np.arange(RIGHT) - REACH
    columns[COLS + RIGHT : COLS + RIM] = np.arange(RIGHT) + COLS - 2 * REACH
    window = np.zeros((WINDOW, 2 * COLS), np.float32)
    for j, column in enumerate(columns):
        if column > -1000:
            centre = column // 2 + MARGIN
            window[centre, j] = 0.75
            window[centre - 1 + 2 * (column % 2), j] = 0.25
    pair = []
    for part in (window[:HALF], window[HALF:]):
        table = np.zeros((COLS, 4 * COLS), np.float32)
        table[:WINDOW, : 2 * COLS] = window
        table[WINDOW : WINDOW + HALF, 2 * COLS :] = part
        pair.append(np.concatenate((table, table), axis=0).astype(ml_dtypes.bfloat16))
    return pair


def call(kernel, outputs, scratch=(), limit=48, microseconds=1, copies=0):
    specs = {"in_specs": [pl.BlockSpec(memory_space=pltpu.HBM)] * copies} if copies else {}
    return pl.pallas_call(
        kernel,
        out_shape=[jax.ShapeDtypeStruct(shape, F32) for shape in outputs],
        **specs,
        scratch_shapes=[pltpu.VMEM(shape, F32) for shape in scratch]
        + ([pltpu.SemaphoreType.DMA((copies,))] if copies else []),
        compiler_params=pltpu.CompilerParams(vmem_limit_bytes=limit * 2**20),
        cost_estimate=pl.CostEstimate(
            flops=0, bytes_accessed=3_000_000 * microseconds, transcendentals=0
        ),
    )


def local(les_wind, les_temp, acoustic_start):
    block = (LEVELS, COLS)
    groups = lax.axis_size("gy")
    packed, tile, x_near, x_far, y_near, y_far = call(
        pack_kernel,
        [(groups, 2, 2) + block, (3, ROWS) + block]
        + 2 * [(3, REACH) + block]
        + 2 * [(3, SIDE) + block],
        scratch=[les_wind.shape, les_temp.shape, (3 * LEVELS * ROWS, COLS)],
        copies=3,
        limit=PACK_LIMIT,
    )(les_wind, les_temp, acoustic_start.reshape(3 * LEVELS * ROWS, COLS))
    coarse = lax.all_to_all(packed, "gy", split_axis=0, concat_axis=0, tiled=True)
    coarse = coarse.reshape((CROWS, 2) + block)
    y_near, y_far = swap_near(y_near, "gy"), swap_far(y_far, "gy")
    x_near, x_far = swap_near(x_near, "gx"), swap_far(x_far, "gx")
    s_near, s_far = call(second_pack_kernel, 2 * [(2 * HROWS + 3 * CREGS,) + block])(
        coarse, y_near, y_far
    )
    s_near, s_far = swap_near(s_near, "gx"), swap_far(s_far, "gx")
    east_table, north_table = (jnp.asarray(table) for table in tables())
    table = jnp.asarray(difference_table())
    edges, inside, refined = call(
        inner_kernel,
        [(STAGES, 2, 3, 2 * HAND) + block, (3, ROWS - 2 * REACH) + block, (2, 3, CROWS) + block],
        scratch=4 * [(2, 3, ROWS) + block],
        microseconds=6,
    )(coarse, tile, y_near, y_far, east_table, north_table, table)
    (end,) = call(
        outer_kernel,
        [(3 * LEVELS * ROWS, COLS)],
        scratch=[(2, 3, 2 * (MARGIN + HROWS)) + block, (2, 2, 3, 2 * (MARGIN + HROWS)) + block]
        + 3 * [(2, 2, 3, 2 * REACH) + block],
        microseconds=6,
    )(x_near, x_far, s_near, s_far, edges, inside, refined, east_table, north_table, table)
    return end.reshape(acoustic_start.shape)


def solution(mesh):
    in_specs = (
        P(None, None, ("gx", "gy"), None),
        P(None, ("gx", "gy"), None),
        P(None, None, "gx", "gy"),
    )
    out_specs = P(None, None, "gx", "gy")
    return jax.shard_map(local, mesh=mesh, in_specs=in_specs, out_specs=out_specs, check_vma=False)
```

```python
import jax
import jax.numpy as jnp
from jax import lax
from jax.experimental import pallas as pl
from jax.experimental.pallas import tpu as pltpu
from jax.sharding import PartitionSpec as P

STEPS = 3
STAGES = 3 * STEPS
REACH = 2 * STAGES
LEVELS = 8
ROWS = 64
COLS = 128
EXT = ROWS + 2 * REACH
MARGIN = REACH // 2 + 1
CROWS = ROWS // 2
WINDOW = COLS // 2 + 2 * MARGIN
HALF = WINDOW // 2
RIGHT = 3 * REACH
RIM = 6 * REACH
EDGE = REACH // 3
MIDDLE = (ROWS - 2 * REACH) // 7
HROWS = REACH // 2
PAIRS = REACH // 2
PER = COLS // REACH
CREGS = -(-2 * PAIRS // PER)
HAND = 6
CHUNK = 16
PACK_LIMIT = 60
SIDE = EDGE + MIDDLE

time_step = 0.4
scale = time_step / 12.0

F32 = jnp.float32


def lanes():
    return lax.broadcasted_iota(jnp.int32, (LEVELS, COLS), 1)


def parity(axis):
    return lax.rem(lax.axis_index(axis), 2)


def swap_near(values, axis):
    return lax.ppermute(values, axis, [(i, i ^ 1) for i in range(lax.axis_size(axis))])


def swap_far(values, axis):
    count = lax.axis_size(axis)
    return lax.ppermute(
        values, axis, [(i, (i + 1) % count if i % 2 else (i - 1) % count) for i in range(count)]
    )


def roll(values, shift):
    if isinstance(shift, int):
        shift = shift % COLS
        if shift == 0:
            return values
    return pltpu.roll(values, shift, values.ndim - 1)


def slots():
    pieces = []
    for k in range(3):
        pieces.append((EDGE * k, EDGE, 0, k))
        pieces.append((ROWS - REACH + EDGE * k, EDGE, 0, 3 + k))
    for k in range(7):
        pieces.append((REACH + MIDDLE * k, MIDDLE, EDGE, k))
    return pieces


def pack_coarse(wind_ref, temp_ref, out_ref):
    lane = lanes()
    blocks = wind_ref.shape[-1] // COLS

    def windows(values):
        parts = [values[:, COLS * i : COLS * (i + 1)] for i in range(blocks)]
        near = [roll(part, MARGIN) for part in parts]
        far = [roll(part, COLS // 2 + MARGIN) for part in parts]
        result = []
        for i in range(blocks):
            result.append(jnp.where(lane < MARGIN, near[i - 1], near[i]))
            result.append(jnp.where(lane < COLS // 2 + MARGIN, far[i], far[(i + 1) % blocks]))
        return result

    for row in range(2):
        east = windows(wind_ref[0, :, row, :])
        north = windows(wind_ref[1, :, row, :])
        warm = windows(temp_ref[:, row, :])
        for j in range(2 * blocks):
            out_ref[j, row, 0] = jnp.where(lane < WINDOW, east[j], roll(warm[j], WINDOW))
            out_ref[j, row, 1] = jnp.where(lane < WINDOW, north[j], roll(warm[j], HALF))


def pack_kernel(
    wind_hbm, temp_hbm, start_hbm, out_ref, tile_ref, x_near_ref, x_far_ref, y_near_ref, y_far_ref,
    wind_ref, temp_ref, start_ref, sems,
):
    x_odd, y_odd = parity("gx"), parity("gy")
    wind_copy = pltpu.make_async_copy(wind_hbm, wind_ref, sems.at[0])
    temp_copy = pltpu.make_async_copy(temp_hbm, temp_ref, sems.at[1])
    start_copy = pltpu.make_async_copy(start_hbm, start_ref, sems.at[2])
    wind_copy.start()
    temp_copy.start()
    start_copy.start()
    wind_copy.wait()
    temp_copy.wait()
    pack_coarse(wind_ref, temp_ref, out_ref)
    start_copy.wait()
    for f in range(3):
        for row in range(ROWS):
            tile_ref[f, row] = start_ref[pl.ds(f * LEVELS * ROWS + row, LEVELS, stride=ROWS), :]
    x_near_ref[...] = tile_ref[:, pl.ds((1 - x_odd) * (ROWS - REACH), REACH)]
    x_far_ref[...] = tile_ref[:, pl.ds(x_odd * (ROWS - REACH), REACH)]
    lane = lanes()
    for ref, first in (
        (y_near_ref, (1 - y_odd) * (COLS - REACH)),
        (y_far_ref, y_odd * (COLS - REACH)),
    ):
        for f in range(3):
            for size, base in ((EDGE, 0), (MIDDLE, EDGE)):
                packed = None
                for row, count, register, slot in slots():
                    if register != base:
                        continue
                    shift = lax.rem(REACH * slot - first + COLS, COLS)
                    moved = roll(tile_ref[f, row : row + count], shift)
                    if packed is None:
                        packed = moved
                    else:
                        inside = (lane >= REACH * slot) & (lane < REACH * (slot + 1))
                        packed = jnp.where(inside, moved, packed)
                ref[f, base : base + size] = packed


def corner_slot(away, right):
    pair = min(away, REACH - 2 - away)
    register, slot = divmod(pair + PAIRS * right, PER)
    offset = 0
    if away > pair:
        offset = (REACH - 1 - pair) * (1 if right else -1)
    return register, REACH * slot, offset


def corner_lanes(away, right, lane):
    _, first, _ = corner_slot(away, right)
    pair = min(away, REACH - 2 - away)
    if away == pair:
        low, high = (0, REACH - 1 - away) if right else (1 + away, REACH)
    else:
        low, high = (REACH - 1 - pair, REACH) if right else (0, pair + 1)
    return (lane >= first + low) & (lane < first + high)


def second_pack_kernel(coarse_ref, y_near_ref, y_far_ref, x_near_ref, x_far_ref):
    x_odd, y_odd = parity("gx"), parity("gy")
    lane = lanes()
    for ref, bottom in ((x_near_ref, 1 - x_odd), (x_far_ref, x_odd)):
        first = bottom * (CROWS - HROWS)
        for i in range(HROWS):
            for c in range(2):
                ref[2 * i + c] = coarse_ref[first + i, c]
        for f in range(3):
            packed = [None] * CREGS
            for away in range(REACH - 1):
                slot, t = divmod(away, EDGE)
                register = t + bottom * (EDGE - 1 - 2 * t)
                source = REACH * (slot + bottom * (5 - 2 * slot))
                for right in range(2):
                    target, start, offset = corner_slot(away, right)
                    take_far = y_odd if right else 1 - y_odd
                    near = y_near_ref[f, register]
                    far = y_far_ref[f, register]
                    halo = jnp.where(jnp.full_like(lane, take_far) == 1, far, near)
                    moved = roll(halo, lax.rem(start + offset - source + 3 * COLS, COLS))
                    if packed[target] is None:
                        packed[target] = moved
                    else:
                        inside = corner_lanes(away, right, lane)
                        packed[target] = jnp.where(inside, moved, packed[target])
            for target in range(CREGS):
                ref[2 * HROWS + CREGS * f + target] = packed[target]


def rim_of(main, left, right, lane):
    own = jnp.where(lane < RIGHT, roll(main, REACH), roll(main, RIGHT - (COLS - 2 * REACH)))
    own = jnp.where(lane < REACH, left, own)
    return jnp.where(lane >= RIM - REACH, right, own)


def products(blocks, table):
    counts = [block.shape[0] * LEVELS for block in blocks]
    values = jnp.concatenate(
        [block.reshape(count, COLS) for block, count in zip(blocks, counts)], axis=0
    )
    high = values.astype(jnp.bfloat16)
    low = (values - high.astype(F32)).astype(jnp.bfloat16)
    result = jnp.dot(
        jnp.concatenate((high, low), axis=1),
        jnp.concatenate((table, table), axis=0),
        preferred_element_type=F32,
    )
    pieces, start = [], 0
    for count in counts:
        pieces.append(result[start : start + count])
        start += count
    return pieces


def stage_products(jobs, table):
    return products([rows[2:-2] for source, _, _, _ in jobs for rows in source], table)


def stage_sums(jobs, across, stage):
    for index, (source, base, background, store) in enumerate(jobs):
        mid = [rows[2:-2] for rows in source]
        count = mid[0].shape[0]
        dy = [across[3 * index + f].reshape(mid[0].shape) for f in range(3)]
        dx = [
            8.0 * (rows[3 : 3 + count] - rows[1 : 1 + count]) - (rows[4:] - rows[:count])
            for rows in source
        ]
        east, north, warm = background
        change = (
            east * dx[0] + north * dy[0] + scale * (dx[1] + dy[2]),
            east * dx[1] + north * dy[1] + warm * dx[0],
            east * dx[2] + north * dy[2] + warm * dy[0],
        )
        for f in range(3):
            moved = mid[f] - change[f]
            if stage == 1:
                moved = 0.75 * base[f] + 0.25 * moved
            elif stage == 2:
                moved = (1.0 / 3.0) * base[f] + (2.0 / 3.0) * moved
            store(f, moved)


def refine_columns(values, east_table, north_table, store):
    n = values.shape[0]
    (first,) = products([values[:, 0]], east_table)
    (second,) = products([values[:, 1]], north_table)
    warm = first[:, 2 * COLS :] + second[:, 2 * COLS :]
    for k in range(2):
        cut = slice(COLS * k, COLS * (k + 1))
        for f, result in enumerate((first, second, warm)):
            store(k, f, result[:, cut].reshape(n, LEVELS, COLS))


def merged(main, rim, lane):
    value = jnp.where(lane < REACH, roll(rim, -REACH), main)
    return jnp.where(lane >= COLS - REACH, roll(rim, COLS - 2 * REACH - RIGHT), value)


def compose_kernel(tile_ref, y_near_ref, y_far_ref, state_ref):
    y_odd = parity("gy")
    lane = lanes()
    take_near = (lane >= RIGHT).astype(jnp.int32) == 1 - y_odd
    state_ref[0] = tile_ref[...]
    for row, count, register, slot in slots():
        near_shift = lax.rem((1 - y_odd) * (RIM - REACH) - REACH * slot + COLS, COLS)
        far_shift = lax.rem(y_odd * (RIM - REACH) - REACH * slot + COLS, COLS)
        for f in range(3):
            near = roll(y_near_ref[f, register : register + count], near_shift)
            far = roll(y_far_ref[f, register : register + count], far_shift)
            halo = jnp.where(take_near, near, far)
            main = tile_ref[f, row : row + count]
            state_ref[1, f, row : row + count] = rim_of(main, halo, halo, lane)


def inner_kernel(
    coarse_ref, start_ref, edges_ref, inside_ref, refined_ref,
    background, state, first, second,
):
    lane = lanes()
    east_table, north_table, table = refine_table(0), refine_table(1), difference_table()

    for start in range(0, CROWS, CHUNK):

        def keep(k, f, values, start=start):
            refined_ref[k, f, start : start + CHUNK] = values

        refine_columns(coarse_ref[start : start + CHUNK], east_table, north_table, keep)
    for k in range(2):
        for f in range(3):
            refine_rows(refined_ref, k, f, 0, CROWS, background, 0)

    for s in range(STAGES):
        origin = start_ref if s < 3 else state
        buffers = (origin, first, second, state)
        source, target = buffers[s % 3], buffers[s % 3 + 1]
        for c in range(2):
            for f in range(3):
                edges_ref[s, c, f, :HAND] = source[c, f, 2 * s : 2 * s + HAND]
                edges_ref[s, c, f, HAND:] = source[c, f, ROWS - 2 * s - HAND : ROWS - 2 * s]
        low, top = 2 * (s + 1), ROWS - 2 * (s + 1)
        for start in range(low, top, CHUNK):
            stop = min(start + CHUNK, top)
            jobs = []
            for c in range(2):

                def store(f, values, c=c):
                    target[c, f, start:stop] = values

                jobs.append((
                    [source[c, f, start - 2 : stop + 2] for f in range(3)],
                    [origin[c, f, start:stop] for f in range(3)],
                    [background[c, f, start:stop] for f in range(3)],
                    store,
                ))
            stage_sums(jobs, stage_products(jobs, table), s % 3)
    for f in range(3):
        rows = slice(REACH, ROWS - REACH)
        inside_ref[f] = merged(state[0, f, rows], state[1, f, rows], lane)


def refine_rows(refined, k, f, start, count, background, first):
    block = refined[k, f, start : start + count]
    centre = (0.75 * scale) * block
    side = (0.25 * scale) * block
    odd = centre[:-1] + side[1:]
    even = centre[1:] + side[:-1]
    for i in range(count - 1):
        background[k, f, first + 2 * i + 1] = odd[i]
        background[k, f, first + 2 * i + 2] = even[i]


def outer_end(
    side, main_ref, message_ref, edges_ref, refined_ref, refined, background, state, first, second
):
    lane = lanes()
    east_table, north_table, table = refine_table(0), refine_table(1), difference_table()
    own = MARGIN + HROWS
    for k in range(2):
        for f in range(3):
            refined[k, f, pl.ds((1 - side) * HROWS, MARGIN)] = refined_ref[
                k, f, pl.ds(side * (CROWS - MARGIN), MARGIN)
            ]

    def keep(k, f, values):
        refined[k, f, pl.ds(side * MARGIN, HROWS)] = values

    values = message_ref[: 2 * HROWS].reshape(HROWS, 2, LEVELS, COLS)
    refine_columns(values, east_table, north_table, keep)
    for k in range(2):
        for f in range(3):
            refine_rows(refined, k, f, 0, own, background, 0)

    halo = side * (REACH + HAND)
    for f in range(3):
        state[0, f, pl.ds(halo, REACH)] = main_ref[f]
        for away in range(REACH):
            row = REACH - 1 - away + side * (2 * away - REACH + 1)
            sides = []
            for right in range(2):
                register, start, offset = corner_slot(min(away, REACH - 2), right)
                corner = message_ref[2 * HROWS + CREGS * f + register]
                sides.append(roll(corner, (RIM - REACH) * right - start - offset))
            state[1, f, halo + row] = rim_of(main_ref[f, row], sides[0], sides[1], lane)

    buffers = (state, first, second, state)

    def job_of(c, s):
        source, target = buffers[s % 3], buffers[s % 3 + 1]
        low = 2 * (s + 1) + side * (REACH + 2 - 4 * s)
        handed = REACH + 2 * s - side * 4 * s
        for f in range(3):
            source[c, f, pl.ds(handed, HAND)] = edges_ref[s, c, f, pl.ds(side * HAND, HAND)]

        def store(f, values):
            target[c, f, pl.ds(low, REACH)] = values

        return (
            [source[c, f, pl.ds(low - 2, REACH + 4)] for f in range(3)],
            [state[c, f, pl.ds(low, REACH)] for f in range(3)],
            [background[c, f, pl.ds(low - 4 * side, REACH)] for f in range(3)],
            store,
        )

    waiting = [None, None]
    for s in range(STAGES + 1):
        for c in range(2):
            if waiting[c] is not None:
                stage_sums(waiting[c][0], waiting[c][1], (s - 1) % 3)
            if s < STAGES:
                jobs = [job_of(c, s)]
                waiting[c] = (jobs, stage_products(jobs, table))
    rows = pl.ds(REACH - 2 * HAND * side, REACH)
    return [merged(state[0, f, rows], state[1, f, rows], lane) for f in range(3)]


def near_end_kernel(
    main_ref, message_ref, edges_ref, refined_ref, end_ref, refined, background, state, first, second
):
    side = 1 - parity("gx")
    ends = outer_end(
        side, main_ref, message_ref, edges_ref, refined_ref, refined, background, state, first, second
    )
    for f in range(3):
        end_ref[f] = ends[f]


def far_end_kernel(
    main_ref, message_ref, edges_ref, refined_ref, near_ref, inside_ref, out_ref,
    refined, background, state, first, second,
):
    side = parity("gx")
    for f in range(3):
        for row in range(ROWS - 2 * REACH):
            at = f * LEVELS * ROWS + REACH + row
            out_ref[pl.ds(at, LEVELS, stride=ROWS), :] = inside_ref[f, row]
        for row in range(REACH):
            at = f * LEVELS * ROWS + row + (1 - side) * (ROWS - REACH)
            out_ref[pl.ds(at, LEVELS, stride=ROWS), :] = near_ref[f, row]
    ends = outer_end(
        side, main_ref, message_ref, edges_ref, refined_ref, refined, background, state, first, second
    )
    for f in range(3):
        for row in range(REACH):
            at = f * LEVELS * ROWS + row + side * (ROWS - REACH)
            out_ref[pl.ds(at, LEVELS, stride=ROWS), :] = ends[f][row]


def refine_table(north):
    row = lax.broadcasted_iota(jnp.int32, (COLS, 2 * COLS), 0)
    lane = lax.broadcasted_iota(jnp.int32, (COLS, 2 * COLS), 1)
    rim = lane - COLS
    column = jnp.where(rim < RIGHT, rim - REACH, rim - RIGHT + COLS - 2 * REACH)
    column = jnp.where(lane < COLS, lane, column)
    centre = lax.shift_right_arithmetic(column, 1) + MARGIN
    side = centre - 1 + 2 * (column & 1)

    def weights(window, used):
        weight = jnp.where(window == centre, 0.75, jnp.where(window == side, 0.25, 0.0))
        return jnp.where(used & (rim < RIM), weight, 0.0).astype(jnp.bfloat16)

    wind = weights(row, row < WINDOW)
    warm = weights(row - WINDOW + HALF * north, (row >= WINDOW) & (row < WINDOW + HALF))
    return jnp.concatenate((wind, warm), axis=1)


def difference_table():
    source = lax.broadcasted_iota(jnp.int32, (COLS, COLS), 0)
    lane = lax.broadcasted_iota(jnp.int32, (COLS, COLS), 1)
    ahead = (source - lane) & (COLS - 1)
    table = jnp.where(ahead == 1, 8.0, 0.0) - jnp.where(ahead == COLS - 1, 8.0, 0.0)
    table = table - jnp.where(ahead == 2, 1.0, 0.0) + jnp.where(ahead == COLS - 2, 1.0, 0.0)
    return table.astype(jnp.bfloat16)


def call(
    kernel, outputs, scratch=(), limit=48, microseconds=1, fetched=(), sent=False, semaphores=0
):
    here, there = pl.BlockSpec(memory_space=pltpu.VMEM), pl.BlockSpec(memory_space=pltpu.HBM)

    def run(*operands):
        return pl.pallas_call(
            kernel,
            out_shape=[jax.ShapeDtypeStruct(shape, F32) for shape in outputs],
            in_specs=[there if i in fetched else here for i in range(len(operands))],
            out_specs=[there if sent else here] * len(outputs),
            scratch_shapes=[pltpu.VMEM(shape, F32) for shape in scratch]
            + ([pltpu.SemaphoreType.DMA((semaphores,))] if semaphores else []),
            compiler_params=pltpu.CompilerParams(vmem_limit_bytes=limit * 2**20),
            cost_estimate=pl.CostEstimate(
                flops=0, bytes_accessed=3_000_000 * microseconds, transcendentals=0
            ),
        )(*operands)

    return run


def local(les_wind, les_temp, acoustic_start):
    block = (LEVELS, COLS)
    groups = lax.axis_size("gy")
    packed, tile, x_near, x_far, y_near, y_far = call(
        pack_kernel,
        [(groups, 2, 2) + block, (3, ROWS) + block]
        + 2 * [(3, REACH) + block]
        + 2 * [(3, SIDE) + block],
        scratch=[les_wind.shape, les_temp.shape, (3 * LEVELS * ROWS, COLS)],
        fetched=(0, 1, 2),
        semaphores=3,
        limit=PACK_LIMIT,
    )(les_wind, les_temp, acoustic_start.reshape(3 * LEVELS * ROWS, COLS))
    coarse = lax.all_to_all(packed, "gy", split_axis=0, concat_axis=0, tiled=True)
    coarse = coarse.reshape((CROWS, 2) + block)
    x_near, x_far = swap_near(x_near, "gx"), swap_far(x_far, "gx")
    y_near, y_far = swap_near(y_near, "gy"), swap_far(y_far, "gy")
    s_near, s_far = call(second_pack_kernel, 2 * [(2 * HROWS + 3 * CREGS,) + block])(
        coarse, y_near, y_far
    )
    s_near, s_far = swap_near(s_near, "gx"), swap_far(s_far, "gx")
    (state,) = call(compose_kernel, [(2, 3, ROWS) + block])(tile, y_near, y_far)
    edges, inside, refined = call(
        inner_kernel,
        [(STAGES, 2, 3, 2 * HAND) + block, (3, ROWS - 2 * REACH) + block, (2, 3, CROWS) + block],
        scratch=4 * [(2, 3, ROWS) + block],
        microseconds=6,
    )(coarse, state)
    scratch = [(2, 3, MARGIN + HROWS) + block, (2, 3, 2 * (MARGIN + HROWS)) + block]
    scratch += 3 * [(2, 3, REACH + REACH + HAND) + block]
    (near,) = call(near_end_kernel, [(3, REACH) + block], scratch=scratch, microseconds=3)(
        x_near, s_near, edges, refined
    )
    (end,) = call(far_end_kernel, [(3 * LEVELS * ROWS, COLS)], scratch=scratch, microseconds=3)(
        x_far, s_far, edges, refined, near, inside
    )
    return end.reshape(acoustic_start.shape)


def solution(mesh):
    in_specs = (
        P(None, None, ("gx", "gy"), None),
        P(None, ("gx", "gy"), None),
        P(None, None, "gx", "gy"),
    )
    out_specs = P(None, None, "gx", "gy")
    return jax.shard_map(local, mesh=mesh, in_specs=in_specs, out_specs=out_specs, check_vma=False)
```

```python
import jax
import jax.numpy as jnp
from jax import lax
from jax.experimental import pallas as pl
from jax.experimental.pallas import tpu as pltpu
from jax.sharding import PartitionSpec as P

STEPS = 3
STAGES = 3 * STEPS
REACH = 2 * STAGES
LEVELS = 8
ROWS = 64
COLS = 128
EXT = ROWS + 2 * REACH
MARGIN = REACH // 2 + 1
CROWS = ROWS // 2
WINDOW = COLS // 2 + 2 * MARGIN
HALF = WINDOW // 2
RIGHT = 3 * REACH
RIM = 6 * REACH
EDGE = REACH // 3
MIDDLE = (ROWS - 2 * REACH) // 7
HROWS = REACH // 2
PAIRS = REACH // 2
PER = COLS // REACH
CREGS = -(-2 * PAIRS // PER)
OWN = -(-REACH // 8) * 8
HAND = 6
CHUNK = 16
PACK_LIMIT = 57
SIDE = EDGE + MIDDLE

time_step = 0.4
scale = time_step / 12.0

F32 = jnp.float32


def lanes():
    return lax.broadcasted_iota(jnp.int32, (LEVELS, COLS), 1)


def parity(axis):
    return lax.rem(lax.axis_index(axis), 2)


def swap_near(values, axis):
    return lax.ppermute(values, axis, [(i, i ^ 1) for i in range(lax.axis_size(axis))])


def swap_far(values, axis):
    count = lax.axis_size(axis)
    return lax.ppermute(
        values, axis, [(i, (i + 1) % count if i % 2 else (i - 1) % count) for i in range(count)]
    )


def roll(values, shift):
    if isinstance(shift, int):
        shift = shift % COLS
        if shift == 0:
            return values
    return pltpu.roll(values, shift, values.ndim - 1)


def slots():
    pieces = []
    for k in range(3):
        pieces.append((EDGE * k, EDGE, 0, k))
        pieces.append((ROWS - REACH + EDGE * k, EDGE, 0, 3 + k))
    for k in range(7):
        pieces.append((REACH + MIDDLE * k, MIDDLE, EDGE, k))
    return pieces


def pack_coarse(wind_ref, temp_ref, out_ref):
    lane = lanes()
    blocks = wind_ref.shape[-1] // COLS

    def windows(values):
        parts = [values[:, COLS * i : COLS * (i + 1)] for i in range(blocks)]
        near = [roll(part, MARGIN) for part in parts]
        far = [roll(part, COLS // 2 + MARGIN) for part in parts]
        result = []
        for i in range(blocks):
            result.append(jnp.where(lane < MARGIN, near[i - 1], near[i]))
            result.append(jnp.where(lane < COLS // 2 + MARGIN, far[i], far[(i + 1) % blocks]))
        return result

    for row in range(2):
        east = windows(wind_ref[0, :, row, :])
        north = windows(wind_ref[1, :, row, :])
        warm = windows(temp_ref[:, row, :])
        for j in range(2 * blocks):
            out_ref[j, row, 0] = jnp.where(lane < WINDOW, east[j], roll(warm[j], WINDOW))
            out_ref[j, row, 1] = jnp.where(lane < WINDOW, north[j], roll(warm[j], HALF))


def strip_kernel(wind_hbm, temp_hbm, packed_ref, wind_ref, temp_ref, sems):
    wind_copy = pltpu.make_async_copy(wind_hbm, wind_ref, sems.at[0])
    temp_copy = pltpu.make_async_copy(temp_hbm, temp_ref, sems.at[1])
    wind_copy.start()
    temp_copy.start()
    wind_copy.wait()
    temp_copy.wait()
    pack_coarse(wind_ref, temp_ref, packed_ref)


def tile_kernel(start_ref, tile_ref, x_near_ref, x_far_ref, y_near_ref, y_far_ref):
    x_odd, y_odd = parity("gx"), parity("gy")
    for f in range(3):
        for row in range(ROWS):
            values = start_ref[pl.ds(f * LEVELS * ROWS + row, LEVELS, stride=ROWS), :]
            tile_ref[f, row] = values * (1.0 / scale) if f == 0 else values
    x_near_ref[...] = tile_ref[:, pl.ds((1 - x_odd) * (ROWS - REACH), REACH)]
    x_far_ref[...] = tile_ref[:, pl.ds(x_odd * (ROWS - REACH), REACH)]
    lane = lanes()
    for ref, first in (
        (y_near_ref, (1 - y_odd) * (COLS - REACH)),
        (y_far_ref, y_odd * (COLS - REACH)),
    ):
        for f in range(3):
            for size, base in ((EDGE, 0), (MIDDLE, EDGE)):
                packed = None
                for row, count, register, slot in slots():
                    if register != base:
                        continue
                    shift = lax.rem(REACH * slot - first + COLS, COLS)
                    moved = roll(tile_ref[f, row : row + count], shift)
                    if packed is None:
                        packed = moved
                    else:
                        inside = (lane >= REACH * slot) & (lane < REACH * (slot + 1))
                        packed = jnp.where(inside, moved, packed)
                ref[f, base : base + size] = packed


def corner_slot(away, right):
    pair = min(away, REACH - 2 - away)
    register, slot = divmod(pair + PAIRS * right, PER)
    offset = 0
    if away > pair:
        offset = (REACH - 1 - pair) * (1 if right else -1)
    return register, REACH * slot, offset


def corner_lanes(away, right, lane):
    _, first, _ = corner_slot(away, right)
    pair = min(away, REACH - 2 - away)
    if away == pair:
        low, high = (0, REACH - 1 - away) if right else (1 + away, REACH)
    else:
        low, high = (REACH - 1 - pair, REACH) if right else (0, pair + 1)
    return (lane >= first + low) & (lane < first + high)


def second_pack_kernel(coarse_ref, y_near_ref, y_far_ref, x_near_ref, x_far_ref):
    x_odd, y_odd = parity("gx"), parity("gy")
    lane = lanes()
    for ref, bottom in ((x_near_ref, 1 - x_odd), (x_far_ref, x_odd)):
        first = bottom * (CROWS - HROWS)
        for i in range(HROWS):
            for c in range(2):
                ref[2 * i + c] = coarse_ref[first + i, c]
        for f in range(3):
            packed = [None] * CREGS
            for away in range(REACH - 1):
                slot, t = divmod(away, EDGE)
                register = t + bottom * (EDGE - 1 - 2 * t)
                source = REACH * (slot + bottom * (5 - 2 * slot))
                for right in range(2):
                    target, start, offset = corner_slot(away, right)
                    take_far = y_odd if right else 1 - y_odd
                    near = y_near_ref[f, register]
                    far = y_far_ref[f, register]
                    halo = jnp.where(jnp.full_like(lane, take_far) == 1, far, near)
                    moved = roll(halo, lax.rem(start + offset - source + 3 * COLS, COLS))
                    if packed[target] is None:
                        packed[target] = moved
                    else:
                        inside = corner_lanes(away, right, lane)
                        packed[target] = jnp.where(inside, moved, packed[target])
            for target in range(CREGS):
                ref[2 * HROWS + CREGS * f + target] = packed[target]


def rim_of(main, left, right, lane):
    own = jnp.where(lane < RIGHT, roll(main, REACH), roll(main, RIGHT - (COLS - 2 * REACH)))
    own = jnp.where(lane < REACH, left, own)
    return jnp.where(lane >= RIM - REACH, right, own)


def products(blocks, table):
    counts = [block.shape[0] * LEVELS for block in blocks]
    values = jnp.concatenate(
        [block.reshape(count, COLS) for block, count in zip(blocks, counts)], axis=0
    )
    high = values.astype(jnp.bfloat16)
    low = (values - high.astype(F32)).astype(jnp.bfloat16)
    result = jnp.dot(
        jnp.concatenate((high, low), axis=1),
        jnp.concatenate((table, table), axis=0),
        preferred_element_type=F32,
    )
    pieces, start = [], 0
    for count in counts:
        pieces.append(result[start : start + count])
        start += count
    return pieces


def stage_products(jobs, table):
    return products([rows[2:-2] for source, _, _, _ in jobs for rows in source], table)


def stage_sums(jobs, across, stage):
    for index, (source, base, background, store) in enumerate(jobs):
        mid = [rows[2:-2] for rows in source]
        count = mid[0].shape[0]
        dy = [across[3 * index + f].reshape(mid[0].shape) for f in range(3)]
        dx = [
            8.0 * (rows[3 : 3 + count] - rows[1 : 1 + count]) - (rows[4:] - rows[:count])
            for rows in source
        ]
        east, north, warm = background
        change = (
            east * dx[0] + north * dy[0] + (dx[1] + dy[2]),
            east * dx[1] + north * dy[1] + warm * dx[0],
            east * dx[2] + north * dy[2] + warm * dy[0],
        )
        for f in range(3):
            moved = mid[f] - change[f]
            if stage == 0:
                moved = (1.0 / 6.0) * moved
            elif stage == 1:
                moved = 0.5 * base[f] + moved
            else:
                moved = (1.0 / 3.0) * base[f] + moved
            store(f, moved)


def refine_columns(values, east_table, north_table, store):
    n = values.shape[0]
    (first,) = products([values[:, 0]], east_table)
    (second,) = products([values[:, 1]], north_table)
    warm = first[:, 2 * COLS :] + second[:, 2 * COLS :]
    for k in range(2):
        cut = slice(COLS * k, COLS * (k + 1))
        for f, result in enumerate((first, second, warm)):
            store(k, f, result[:, cut].reshape(n, LEVELS, COLS))


def merged(f, main, rim, lane):
    value = jnp.where(lane < REACH, roll(rim, -REACH), main)
    value = jnp.where(lane >= COLS - REACH, roll(rim, COLS - 2 * REACH - RIGHT), value)
    return value * scale if f == 0 else value


def inner_kernel(
    coarse_ref, tile_ref, y_near_ref, y_far_ref, edges_ref, inside_ref, refined_ref,
    background, state, first, second, rim_ref,
):
    y_odd = parity("gy")
    lane = lanes()
    east_table, north_table, table = refine_table(0), refine_table(1), difference_table()

    for start in range(0, CROWS, CHUNK):

        def keep(k, f, values, start=start):
            refined_ref[k, f, start : start + CHUNK] = values

        refine_columns(coarse_ref[start : start + CHUNK], east_table, north_table, keep)
    for k in range(2):
        for f in range(3):
            refine_rows(refined_ref, k, f, 0, CROWS, background, 0)

    take_near = (lane >= RIGHT).astype(jnp.int32) == 1 - y_odd
    for row, count, register, slot in slots():
        near_shift = lax.rem((1 - y_odd) * (RIM - REACH) - REACH * slot + COLS, COLS)
        far_shift = lax.rem(y_odd * (RIM - REACH) - REACH * slot + COLS, COLS)
        for f in range(3):
            near = roll(y_near_ref[f, register : register + count], near_shift)
            far = roll(y_far_ref[f, register : register + count], far_shift)
            halo = jnp.where(take_near, near, far)
            rim_ref[f, row : row + count] = rim_of(tile_ref[f, row : row + count], halo, halo, lane)

    class Start:
        def __getitem__(self, index):
            c, f, rows = index
            return (rim_ref if c else tile_ref)[f, rows]

    start_state = Start()
    for s in range(STAGES):
        origin = start_state if s < 3 else state
        buffers = (origin, first, second, state)
        source, target = buffers[s % 3], buffers[s % 3 + 1]
        for c in range(2):
            for f in range(3):
                edges_ref[s, c, f, :HAND] = source[c, f, 2 * s : 2 * s + HAND]
                edges_ref[s, c, f, HAND:] = source[c, f, ROWS - 2 * s - HAND : ROWS - 2 * s]
        low, top = 2 * (s + 1), ROWS - 2 * (s + 1)
        for start in range(low, top, CHUNK):
            stop = min(start + CHUNK, top)
            jobs = []
            for c in range(2):

                def store(f, values, c=c):
                    target[c, f, start:stop] = values

                jobs.append((
                    [source[c, f, start - 2 : stop + 2] for f in range(3)],
                    [origin[c, f, start:stop] for f in range(3)],
                    [background[c, f, start:stop] for f in range(3)],
                    store,
                ))
            stage_sums(jobs, stage_products(jobs, table), s % 3)
    for f in range(3):
        rows = slice(REACH, ROWS - REACH)
        inside_ref[f] = merged(f, state[0, f, rows], state[1, f, rows], lane)


def refine_rows(refined, k, f, start, count, background, first):
    block = refined[k, f, start : start + count]
    factor = scale * scale if f == 2 else scale
    centre = (0.75 * factor) * block
    side = (0.25 * factor) * block
    odd = centre[:-1] + side[1:]
    even = centre[1:] + side[:-1]
    for i in range(count - 1):
        background[k, f, first + 2 * i + 1] = odd[i]
        background[k, f, first + 2 * i + 2] = even[i]


def outer_end(
    side, main_ref, message_ref, edges_ref, refined_ref, refined, background, state, first, second
):
    lane = lanes()
    east_table, north_table, table = refine_table(0), refine_table(1), difference_table()
    own = MARGIN + HROWS
    for k in range(2):
        for f in range(3):
            refined[k, f, pl.ds((1 - side) * HROWS, MARGIN)] = refined_ref[
                k, f, pl.ds(side * (CROWS - MARGIN), MARGIN)
            ]

    def keep(k, f, values):
        refined[k, f, pl.ds(side * MARGIN, HROWS)] = values

    values = message_ref[: 2 * HROWS].reshape(HROWS, 2, LEVELS, COLS)
    refine_columns(values, east_table, north_table, keep)
    for k in range(2):
        for f in range(3):
            refine_rows(refined, k, f, 0, own, background, 0)

    halo = side * (REACH + HAND)
    for f in range(3):
        state[0, f, pl.ds(halo, REACH)] = main_ref[f]
        for away in range(REACH):
            row = REACH - 1 - away + side * (2 * away - REACH + 1)
            sides = []
            for right in range(2):
                register, start, offset = corner_slot(min(away, REACH - 2), right)
                corner = message_ref[2 * HROWS + CREGS * f + register]
                sides.append(roll(corner, (RIM - REACH) * right - start - offset))
            state[1, f, halo + row] = rim_of(main_ref[f, row], sides[0], sides[1], lane)

    buffers = (state, first, second, state)

    def job_of(c, s):
        source, target = buffers[s % 3], buffers[s % 3 + 1]
        low = 2 * (s + 1) + side * (REACH + 2 - 4 * s)
        handed = REACH + 2 * s - side * 4 * s
        for f in range(3):
            source[c, f, pl.ds(handed, HAND)] = edges_ref[s, c, f, pl.ds(side * HAND, HAND)]

        def store(f, values):
            target[c, f, pl.ds(low, REACH)] = values

        return (
            [source[c, f, pl.ds(low - 2, REACH + 4)] for f in range(3)],
            [state[c, f, pl.ds(low, REACH)] for f in range(3)],
            [background[c, f, pl.ds(low - 4 * side, REACH)] for f in range(3)],
            store,
        )

    waiting = [None, None]
    for s in range(STAGES + 1):
        for c in range(2):
            if waiting[c] is not None:
                stage_sums(waiting[c][0], waiting[c][1], (s - 1) % 3)
            if s < STAGES:
                jobs = [job_of(c, s)]
                waiting[c] = (jobs, stage_products(jobs, table))
    rows = pl.ds(REACH - 2 * HAND * side, REACH)
    return [merged(f, state[0, f, rows], state[1, f, rows], lane) for f in range(3)]


def place(out_ref, f, row, value):
    rows = out_ref.shape[0] // (3 * LEVELS)
    out_ref[pl.ds(f * LEVELS * rows + row, LEVELS, stride=rows), :] = value


def near_end_kernel(
    main_ref, message_ref, edges_ref, refined_ref, inside_ref, end_ref,
    refined, background, state, first, second, out_ref, sem,
):
    side = 1 - parity("gx")
    for f in range(3):
        for row in range(ROWS - 2 * REACH):
            place(out_ref, f, REACH + row, inside_ref[f, row])
    ends = outer_end(
        side, main_ref, message_ref, edges_ref, refined_ref, refined, background, state, first, second
    )
    for f in range(3):
        for row in range(REACH):
            place(out_ref, f, row + side * (ROWS - REACH), ends[f][row])
    source = out_ref.reshape(3 * LEVELS, ROWS, COLS)
    rows = pl.ds(pl.multiple_of(side * OWN, 8), ROWS - OWN)
    copy = pltpu.make_async_copy(source.at[:, rows], end_ref.at[:, rows], sem.at[0])
    copy.start()
    copy.wait()


def far_end_kernel(
    main_ref, message_ref, edges_ref, refined_ref, inside_ref, before_ref, end_ref,
    refined, background, state, first, second, out_ref, sems,
):
    del before_ref
    side = parity("gx")
    spare = OWN - REACH
    for f in range(3):
        for row in range(spare):
            inner = row + side * (ROWS - 2 * REACH - spare)
            place(out_ref, f, row + (1 - side) * REACH, inside_ref[f, inner])
    ends = outer_end(
        side, main_ref, message_ref, edges_ref, refined_ref, refined, background, state, first, second
    )
    target = out_ref.reshape(3 * LEVELS, OWN, COLS)
    rows = pl.ds(pl.multiple_of(side * (ROWS - OWN), 8), OWN)
    copies = []
    for f in range(3):
        for row in range(REACH):
            place(out_ref, f, row + side * spare, ends[f][row])
        field = pl.ds(f * LEVELS, LEVELS)
        copies.append(
            pltpu.make_async_copy(target.at[field], end_ref.at[field, rows], sems.at[f])
        )
        copies[f].start()
    for copy in copies:
        copy.wait()


def refine_table(north):
    row = lax.broadcasted_iota(jnp.int32, (COLS, 2 * COLS), 0)
    lane = lax.broadcasted_iota(jnp.int32, (COLS, 2 * COLS), 1)
    rim = lane - COLS
    column = jnp.where(rim < RIGHT, rim - REACH, rim - RIGHT + COLS - 2 * REACH)
    column = jnp.where(lane < COLS, lane, column)
    centre = lax.shift_right_arithmetic(column, 1) + MARGIN
    side = centre - 1 + 2 * (column & 1)

    def weights(window, used):
        weight = jnp.where(window == centre, 0.75, jnp.where(window == side, 0.25, 0.0))
        return jnp.where(used & (rim < RIM), weight, 0.0).astype(jnp.bfloat16)

    wind = weights(row, row < WINDOW)
    warm = weights(row - WINDOW + HALF * north, (row >= WINDOW) & (row < WINDOW + HALF))
    return jnp.concatenate((wind, warm), axis=1)


def difference_table():
    source = lax.broadcasted_iota(jnp.int32, (COLS, COLS), 0)
    lane = lax.broadcasted_iota(jnp.int32, (COLS, COLS), 1)
    ahead = (source - lane) & (COLS - 1)
    table = jnp.where(ahead == 1, 8.0, 0.0) - jnp.where(ahead == COLS - 1, 8.0, 0.0)
    table = table - jnp.where(ahead == 2, 1.0, 0.0) + jnp.where(ahead == COLS - 2, 1.0, 0.0)
    return table.astype(jnp.bfloat16)


def call(
    kernel, outputs, scratch=(), limit=48, microseconds=1, fetched=(), sent=False, semaphores=0,
    aliases=None,
):
    here, there = pl.BlockSpec(memory_space=pltpu.VMEM), pl.BlockSpec(memory_space=pltpu.HBM)

    def run(*operands):
        return pl.pallas_call(
            kernel,
            out_shape=[jax.ShapeDtypeStruct(shape, F32) for shape in outputs],
            in_specs=[there if i in fetched else here for i in range(len(operands))],
            out_specs=[there if sent else here] * len(outputs),
            scratch_shapes=[pltpu.VMEM(shape, F32) for shape in scratch]
            + ([pltpu.SemaphoreType.DMA((semaphores,))] if semaphores else []),
            input_output_aliases=aliases or {},
            compiler_params=pltpu.CompilerParams(vmem_limit_bytes=limit * 2**20),
            cost_estimate=pl.CostEstimate(
                flops=0, bytes_accessed=3_000_000 * microseconds, transcendentals=0
            ),
        )(*operands)

    return run


def local(les_wind, les_temp, acoustic_start):
    block = (LEVELS, COLS)
    groups = lax.axis_size("gy")
    (packed,) = call(
        strip_kernel,
        [(groups, 2, 2) + block],
        scratch=[les_wind.shape, les_temp.shape],
        fetched=(0, 1),
        semaphores=2,
        limit=PACK_LIMIT,
    )(les_wind, les_temp)
    tile, x_near, x_far, y_near, y_far = call(
        tile_kernel, [(3, ROWS) + block] + 2 * [(3, REACH) + block] + 2 * [(3, SIDE) + block]
    )(acoustic_start.reshape(3 * LEVELS * ROWS, COLS))
    coarse = lax.all_to_all(packed, "gy", split_axis=0, concat_axis=0, tiled=True)
    coarse = coarse.reshape((CROWS, 2) + block)
    x_near, x_far = swap_near(x_near, "gx"), swap_far(x_far, "gx")
    y_near, y_far = swap_near(y_near, "gy"), swap_far(y_far, "gy")
    s_near, s_far = call(second_pack_kernel, 2 * [(2 * HROWS + 3 * CREGS,) + block])(
        coarse, y_near, y_far
    )
    s_near, s_far = swap_near(s_near, "gx"), swap_far(s_far, "gx")
    edges, inside, refined = call(
        inner_kernel,
        [(STAGES, 2, 3, 2 * HAND) + block, (3, ROWS - 2 * REACH) + block, (2, 3, CROWS) + block],
        scratch=4 * [(2, 3, ROWS) + block] + [(3, ROWS) + block],
        microseconds=6,
    )(coarse, tile, y_near, y_far)
    scratch = [(2, 3, MARGIN + HROWS) + block, (2, 3, 2 * (MARGIN + HROWS)) + block]
    scratch += 3 * [(2, 3, REACH + REACH + HAND) + block]
    whole = (3 * LEVELS, ROWS, COLS)
    (near,) = call(
        near_end_kernel,
        [whole],
        scratch=scratch + [(3 * LEVELS * ROWS, COLS)],
        microseconds=3,
        sent=True,
        semaphores=1,
    )(x_near, s_near, edges, refined, inside)
    (end,) = call(
        far_end_kernel,
        [whole],
        scratch=scratch + [(3 * LEVELS * OWN, COLS)],
        microseconds=3,
        fetched=(5,),
        sent=True,
        semaphores=3,
        aliases={5: 0},
    )(x_far, s_far, edges, refined, inside, near)
    return end.reshape(acoustic_start.shape)


def solution(mesh):
    in_specs = (
        P(None, None, ("gx", "gy"), None),
        P(None, ("gx", "gy"), None),
        P(None, None, "gx", "gy"),
    )
    out_specs = P(None, None, "gx", "gy")
    return jax.shard_map(local, mesh=mesh, in_specs=in_specs, out_specs=out_specs, check_vma=False)
```

```python
import jax
import jax.numpy as jnp
from jax import lax
from jax.experimental import pallas as pl
from jax.experimental.pallas import tpu as pltpu
from jax.sharding import PartitionSpec as P

STEPS = 3
STAGES = 3 * STEPS
REACH = 2 * STAGES
LEVELS = 8
ROWS = 64
COLS = 128
EXT = ROWS + 2 * REACH
MARGIN = REACH // 2 + 1
CROWS = ROWS // 2
WINDOW = COLS // 2 + 2 * MARGIN
HALF = WINDOW // 2
RIGHT = 3 * REACH
RIM = 6 * REACH
EDGE = REACH // 3
MIDDLE = (ROWS - 2 * REACH) // 7
HROWS = REACH // 2
PAIRS = REACH // 2
PER = COLS // REACH
CREGS = -(-2 * PAIRS // PER)
OWN = -(-REACH // 8) * 8
HAND = 6
CHUNK = 16
PACK_LIMIT = 57
SIDE = EDGE + MIDDLE

time_step = 0.4
scale = time_step / 12.0

F32 = jnp.float32


def lanes():
    return lax.broadcasted_iota(jnp.int32, (LEVELS, COLS), 1)


def parity(axis):
    return lax.rem(lax.axis_index(axis), 2)


def swap_near(values, axis):
    return lax.ppermute(values, axis, [(i, i ^ 1) for i in range(lax.axis_size(axis))])


def swap_far(values, axis):
    count = lax.axis_size(axis)
    return lax.ppermute(
        values, axis, [(i, (i + 1) % count if i % 2 else (i - 1) % count) for i in range(count)]
    )


def roll(values, shift):
    if isinstance(shift, int):
        shift = shift % COLS
        if shift == 0:
            return values
    return pltpu.roll(values, shift, values.ndim - 1)


def slots():
    pieces = []
    for k in range(3):
        pieces.append((EDGE * k, EDGE, 0, k))
        pieces.append((ROWS - REACH + EDGE * k, EDGE, 0, 3 + k))
    for k in range(7):
        pieces.append((REACH + MIDDLE * k, MIDDLE, EDGE, k))
    return pieces


def pack_coarse(wind_ref, temp_ref, out_ref, sent):
    lane = lanes()
    blocks = wind_ref.shape[-1] // COLS

    def windows(values):
        parts = [values[:, COLS * i : COLS * (i + 1)] for i in range(blocks)]
        near = [roll(part, MARGIN) for part in parts]
        far = [roll(part, COLS // 2 + MARGIN) for part in parts]
        result = []
        for i in range(blocks):
            result.append(jnp.where(lane < MARGIN, near[i - 1], near[i]))
            result.append(jnp.where(lane < COLS // 2 + MARGIN, far[i], far[(i + 1) % blocks]))
        return result

    for row in range(2):
        east = windows(wind_ref[0, :, row, :])
        north = windows(wind_ref[1, :, row, :])
        warm = windows(temp_ref[:, row, :])
        for j in range(2 * blocks):
            out_ref[j, row, 0] = jnp.where(lane < WINDOW, east[j], roll(warm[j], WINDOW))
            out_ref[j, row, 1] = jnp.where(lane < WINDOW, north[j], roll(warm[j], HALF))
        sent[row].start()


def strip_kernel(wind_hbm, temp_hbm, packed_hbm, wind_ref, temp_ref, packed_ref, sems):
    wind_copy = pltpu.make_async_copy(wind_hbm, wind_ref, sems.at[0])
    temp_copy = pltpu.make_async_copy(temp_hbm, temp_ref, sems.at[1])
    wind_copy.start()
    temp_copy.start()
    sent = [
        pltpu.make_async_copy(packed_ref.at[:, row], packed_hbm.at[:, row], sems.at[2 + row])
        for row in range(2)
    ]
    wind_copy.wait()
    temp_copy.wait()
    pack_coarse(wind_ref, temp_ref, packed_ref, sent)
    sent[0].wait()
    sent[1].wait()


def tile_kernel(start_ref, tile_ref, x_near_ref, x_far_ref, y_near_ref, y_far_ref):
    x_odd, y_odd = parity("gx"), parity("gy")
    for f in range(3):
        for row in range(ROWS):
            values = start_ref[pl.ds(f * LEVELS * ROWS + row, LEVELS, stride=ROWS), :]
            tile_ref[f, row] = values * (1.0 / scale) if f == 0 else values
    x_near_ref[...] = tile_ref[:, pl.ds((1 - x_odd) * (ROWS - REACH), REACH)]
    x_far_ref[...] = tile_ref[:, pl.ds(x_odd * (ROWS - REACH), REACH)]
    lane = lanes()
    for ref, first in (
        (y_near_ref, (1 - y_odd) * (COLS - REACH)),
        (y_far_ref, y_odd * (COLS - REACH)),
    ):
        for f in range(3):
            for size, base in ((EDGE, 0), (MIDDLE, EDGE)):
                packed = None
                for row, count, register, slot in slots():
                    if register != base:
                        continue
                    shift = lax.rem(REACH * slot - first + COLS, COLS)
                    moved = roll(tile_ref[f, row : row + count], shift)
                    if packed is None:
                        packed = moved
                    else:
                        inside = (lane >= REACH * slot) & (lane < REACH * (slot + 1))
                        packed = jnp.where(inside, moved, packed)
                ref[f, base : base + size] = packed


def corner_slot(away, right):
    pair = min(away, REACH - 2 - away)
    register, slot = divmod(pair + PAIRS * right, PER)
    offset = 0
    if away > pair:
        offset = (REACH - 1 - pair) * (1 if right else -1)
    return register, REACH * slot, offset


def corner_lanes(away, right, lane):
    _, first, _ = corner_slot(away, right)
    pair = min(away, REACH - 2 - away)
    if away == pair:
        low, high = (0, REACH - 1 - away) if right else (1 + away, REACH)
    else:
        low, high = (REACH - 1 - pair, REACH) if right else (0, pair + 1)
    return (lane >= first + low) & (lane < first + high)


def second_pack_kernel(coarse_ref, y_near_ref, y_far_ref, x_near_ref, x_far_ref):
    x_odd, y_odd = parity("gx"), parity("gy")
    lane = lanes()
    for ref, bottom in ((x_near_ref, 1 - x_odd), (x_far_ref, x_odd)):
        first = bottom * (CROWS - HROWS)
        for i in range(HROWS):
            for c in range(2):
                ref[2 * i + c] = coarse_ref[first + i, c]
        for f in range(3):
            packed = [None] * CREGS
            for away in range(REACH - 1):
                slot, t = divmod(away, EDGE)
                register = t + bottom * (EDGE - 1 - 2 * t)
                source = REACH * (slot + bottom * (5 - 2 * slot))
                for right in range(2):
                    target, start, offset = corner_slot(away, right)
                    take_far = y_odd if right else 1 - y_odd
                    near = y_near_ref[f, register]
                    far = y_far_ref[f, register]
                    halo = jnp.where(jnp.full_like(lane, take_far) == 1, far, near)
                    moved = roll(halo, lax.rem(start + offset - source + 3 * COLS, COLS))
                    if packed[target] is None:
                        packed[target] = moved
                    else:
                        inside = corner_lanes(away, right, lane)
                        packed[target] = jnp.where(inside, moved, packed[target])
            for target in range(CREGS):
                ref[2 * HROWS + CREGS * f + target] = packed[target]


def rim_of(main, left, right, lane):
    own = jnp.where(lane < RIGHT, roll(main, REACH), roll(main, RIGHT - (COLS - 2 * REACH)))
    own = jnp.where(lane < REACH, left, own)
    return jnp.where(lane >= RIM - REACH, right, own)


def products(blocks, table):
    counts = [block.shape[0] * LEVELS for block in blocks]
    values = jnp.concatenate(
        [block.reshape(count, COLS) for block, count in zip(blocks, counts)], axis=0
    )
    high = values.astype(jnp.bfloat16)
    low = (values - high.astype(F32)).astype(jnp.bfloat16)
    result = jnp.dot(
        jnp.concatenate((high, low), axis=1),
        jnp.concatenate((table, table), axis=0),
        preferred_element_type=F32,
    )
    pieces, start = [], 0
    for count in counts:
        pieces.append(result[start : start + count])
        start += count
    return pieces


def stage_products(jobs, table):
    return products([rows[2:-2] for source, _, _, _ in jobs for rows in source], table)


def stage_sums(jobs, across, stage):
    for index, (source, base, background, store) in enumerate(jobs):
        mid = [rows[2:-2] for rows in source]
        count = mid[0].shape[0]
        dy = [across[3 * index + f].reshape(mid[0].shape) for f in range(3)]
        dx = [
            8.0 * (rows[3 : 3 + count] - rows[1 : 1 + count]) - (rows[4:] - rows[:count])
            for rows in source
        ]
        east, north, warm = background
        change = (
            east * dx[0] + north * dy[0] + (dx[1] + dy[2]),
            east * dx[1] + north * dy[1] + warm * dx[0],
            east * dx[2] + north * dy[2] + warm * dy[0],
        )
        for f in range(3):
            moved = mid[f] - change[f]
            if stage == 0:
                moved = (1.0 / 6.0) * moved
            elif stage == 1:
                moved = 0.5 * base[f] + moved
            else:
                moved = (1.0 / 3.0) * base[f] + moved
            store(f, moved)


def refine_columns(values, east_table, north_table, store):
    n = values.shape[0]
    (first,) = products([values[:, 0]], east_table)
    (second,) = products([values[:, 1]], north_table)
    warm = first[:, 2 * COLS :] + second[:, 2 * COLS :]
    for k in range(2):
        cut = slice(COLS * k, COLS * (k + 1))
        for f, result in enumerate((first, second, warm)):
            store(k, f, result[:, cut].reshape(n, LEVELS, COLS))


def merged(f, main, rim, lane):
    value = jnp.where(lane < REACH, roll(rim, -REACH), main)
    value = jnp.where(lane >= COLS - REACH, roll(rim, COLS - 2 * REACH - RIGHT), value)
    return value * scale if f == 0 else value


def inner_kernel(
    coarse_ref, tile_ref, y_near_ref, y_far_ref, edges_ref, inside_ref, refined_ref,
    background, state, first, second, rim_ref,
):
    y_odd = parity("gy")
    lane = lanes()
    east_table, north_table, table = refine_table(0), refine_table(1), difference_table()

    for start in range(0, CROWS, CHUNK):

        def keep(k, f, values, start=start):
            refined_ref[k, f, start : start + CHUNK] = values

        refine_columns(coarse_ref[start : start + CHUNK], east_table, north_table, keep)
    for k in range(2):
        for f in range(3):
            refine_rows(refined_ref, k, f, 0, CROWS, background, 0)

    take_near = (lane >= RIGHT).astype(jnp.int32) == 1 - y_odd
    for row, count, register, slot in slots():
        near_shift = lax.rem((1 - y_odd) * (RIM - REACH) - REACH * slot + COLS, COLS)
        far_shift = lax.rem(y_odd * (RIM - REACH) - REACH * slot + COLS, COLS)
        for f in range(3):
            near = roll(y_near_ref[f, register : register + count], near_shift)
            far = roll(y_far_ref[f, register : register + count], far_shift)
            halo = jnp.where(take_near, near, far)
            rim_ref[f, row : row + count] = rim_of(tile_ref[f, row : row + count], halo, halo, lane)

    class Start:
        def __getitem__(self, index):
            c, f, rows = index
            return (rim_ref if c else tile_ref)[f, rows]

    start_state = Start()
    for s in range(STAGES):
        origin = start_state if s < 3 else state
        buffers = (origin, first, second, state)
        source, target = buffers[s % 3], buffers[s % 3 + 1]
        for c in range(2):
            for f in range(3):
                edges_ref[s, c, f, :HAND] = source[c, f, 2 * s : 2 * s + HAND]
                edges_ref[s, c, f, HAND:] = source[c, f, ROWS - 2 * s - HAND : ROWS - 2 * s]
        low, top = 2 * (s + 1), ROWS - 2 * (s + 1)
        for start in range(low, top, CHUNK):
            stop = min(start + CHUNK, top)
            jobs = []
            for c in range(2):

                def store(f, values, c=c):
                    target[c, f, start:stop] = values

                jobs.append((
                    [source[c, f, start - 2 : stop + 2] for f in range(3)],
                    [origin[c, f, start:stop] for f in range(3)],
                    [background[c, f, start:stop] for f in range(3)],
                    store,
                ))
            stage_sums(jobs, stage_products(jobs, table), s % 3)
    for f in range(3):
        rows = slice(REACH, ROWS - REACH)
        inside_ref[f] = merged(f, state[0, f, rows], state[1, f, rows], lane)


def refine_rows(refined, k, f, start, count, background, first):
    block = refined[k, f, start : start + count]
    factor = scale * scale if f == 2 else scale
    centre = (0.75 * factor) * block
    side = (0.25 * factor) * block
    odd = centre[:-1] + side[1:]
    even = centre[1:] + side[:-1]
    for i in range(count - 1):
        background[k, f, first + 2 * i + 1] = odd[i]
        background[k, f, first + 2 * i + 2] = even[i]


def outer_end(
    side, main_ref, message_ref, edges_ref, refined_ref, refined, background, state, first, second
):
    lane = lanes()
    east_table, north_table, table = refine_table(0), refine_table(1), difference_table()
    own = MARGIN + HROWS
    for k in range(2):
        for f in range(3):
            refined[k, f, pl.ds((1 - side) * HROWS, MARGIN)] = refined_ref[
                k, f, pl.ds(side * (CROWS - MARGIN), MARGIN)
            ]

    def keep(k, f, values):
        refined[k, f, pl.ds(side * MARGIN, HROWS)] = values[:HROWS]

    values = message_ref[: 2 * HROWS + 2].reshape(HROWS + 1, 2, LEVELS, COLS)
    refine_columns(values, east_table, north_table, keep)
    for k in range(2):
        for f in range(3):
            refine_rows(refined, k, f, 0, own, background, 0)

    halo = side * (REACH + HAND)
    for f in range(3):
        state[0, f, pl.ds(halo, REACH)] = main_ref[f]
        for away in range(REACH):
            row = REACH - 1 - away + side * (2 * away - REACH + 1)
            sides = []
            for right in range(2):
                register, start, offset = corner_slot(min(away, REACH - 2), right)
                corner = message_ref[2 * HROWS + CREGS * f + register]
                sides.append(roll(corner, (RIM - REACH) * right - start - offset))
            state[1, f, halo + row] = rim_of(main_ref[f, row], sides[0], sides[1], lane)

    buffers = (state, first, second, state)

    def job_of(c, s):
        source, target = buffers[s % 3], buffers[s % 3 + 1]
        low = 2 * (s + 1) + side * (REACH + 2 - 4 * s)
        handed = REACH + 2 * s - side * 4 * s
        for f in range(3):
            source[c, f, pl.ds(handed, HAND)] = edges_ref[s, c, f, pl.ds(side * HAND, HAND)]

        def store(f, values):
            target[c, f, pl.ds(low, REACH)] = values

        return (
            [source[c, f, pl.ds(low - 2, REACH + 4)] for f in range(3)],
            [state[c, f, pl.ds(low, REACH)] for f in range(3)],
            [background[c, f, pl.ds(low - 4 * side, REACH)] for f in range(3)],
            store,
        )

    waiting = [None, None]
    for s in range(STAGES + 1):
        for c in range(2):
            if waiting[c] is not None:
                stage_sums(waiting[c][0], waiting[c][1], (s - 1) % 3)
            if s < STAGES:
                jobs = [job_of(c, s)]
                waiting[c] = (jobs, stage_products(jobs, table))
    rows = pl.ds(REACH - 2 * HAND * side, REACH)
    return [merged(f, state[0, f, rows], state[1, f, rows], lane) for f in range(3)]


def place(out_ref, f, row, value):
    rows = out_ref.shape[0] // (3 * LEVELS)
    out_ref[pl.ds(f * LEVELS * rows + row, LEVELS, stride=rows), :] = value


def near_end_kernel(
    main_ref, message_ref, edges_ref, refined_ref, inside_ref, end_ref,
    refined, background, state, first, second, out_ref, sem,
):
    side = 1 - parity("gx")
    for f in range(3):
        for row in range(ROWS - 2 * REACH):
            place(out_ref, f, REACH + row, inside_ref[f, row])
    ends = outer_end(
        side, main_ref, message_ref, edges_ref, refined_ref, refined, background, state, first, second
    )
    for f in range(3):
        for row in range(REACH):
            place(out_ref, f, row + side * (ROWS - REACH), ends[f][row])
    source = out_ref.reshape(3 * LEVELS, ROWS, COLS)
    rows = pl.ds(pl.multiple_of(side * OWN, 8), ROWS - OWN)
    copy = pltpu.make_async_copy(source.at[:, rows], end_ref.at[:, rows], sem.at[0])
    copy.start()
    copy.wait()


def far_end_kernel(
    main_ref, message_ref, edges_ref, refined_ref, inside_ref, before_ref, end_ref,
    refined, background, state, first, second, out_ref, sems,
):
    del before_ref
    side = parity("gx")
    spare = OWN - REACH
    for f in range(3):
        for row in range(spare):
            inner = row + side * (ROWS - 2 * REACH - spare)
            place(out_ref, f, row + (1 - side) * REACH, inside_ref[f, inner])
    ends = outer_end(
        side, main_ref, message_ref, edges_ref, refined_ref, refined, background, state, first, second
    )
    target = out_ref.reshape(3 * LEVELS, OWN, COLS)
    rows = pl.ds(pl.multiple_of(side * (ROWS - OWN), 8), OWN)
    copies = []
    for f in range(3):
        for row in range(REACH):
            place(out_ref, f, row + side * spare, ends[f][row])
        field = pl.ds(f * LEVELS, LEVELS)
        copies.append(
            pltpu.make_async_copy(target.at[field], end_ref.at[field, rows], sems.at[f])
        )
        copies[f].start()
    for copy in copies:
        copy.wait()


def refine_table(north):
    row = lax.broadcasted_iota(jnp.int32, (COLS, 2 * COLS), 0)
    lane = lax.broadcasted_iota(jnp.int32, (COLS, 2 * COLS), 1)
    rim = lane - COLS
    column = jnp.where(rim < RIGHT, rim - REACH, rim - RIGHT + COLS - 2 * REACH)
    column = jnp.where(lane < COLS, lane, column)
    centre = lax.shift_right_arithmetic(column, 1) + MARGIN
    side = centre - 1 + 2 * (column & 1)

    def weights(window, used):
        weight = jnp.where(window == centre, 0.75, jnp.where(window == side, 0.25, 0.0))
        return jnp.where(used & (rim < RIM), weight, 0.0).astype(jnp.bfloat16)

    wind = weights(row, row < WINDOW)
    warm = weights(row - WINDOW + HALF * north, (row >= WINDOW) & (row < WINDOW + HALF))
    return jnp.concatenate((wind, warm), axis=1)


def difference_table():
    source = lax.broadcasted_iota(jnp.int32, (COLS, COLS), 0)
    lane = lax.broadcasted_iota(jnp.int32, (COLS, COLS), 1)
    ahead = (source - lane) & (COLS - 1)
    table = jnp.where(ahead == 1, 8.0, 0.0) - jnp.where(ahead == COLS - 1, 8.0, 0.0)
    table = table - jnp.where(ahead == 2, 1.0, 0.0) + jnp.where(ahead == COLS - 2, 1.0, 0.0)
    return table.astype(jnp.bfloat16)


def call(
    kernel, outputs, scratch=(), limit=48, microseconds=1, fetched=(), sent=False, semaphores=0,
    aliases=None,
):
    here, there = pl.BlockSpec(memory_space=pltpu.VMEM), pl.BlockSpec(memory_space=pltpu.HBM)

    def run(*operands):
        return pl.pallas_call(
            kernel,
            out_shape=[jax.ShapeDtypeStruct(shape, F32) for shape in outputs],
            in_specs=[there if i in fetched else here for i in range(len(operands))],
            out_specs=[there if sent else here] * len(outputs),
            scratch_shapes=[pltpu.VMEM(shape, F32) for shape in scratch]
            + ([pltpu.SemaphoreType.DMA((semaphores,))] if semaphores else []),
            input_output_aliases=aliases or {},
            compiler_params=pltpu.CompilerParams(vmem_limit_bytes=limit * 2**20),
            cost_estimate=pl.CostEstimate(
                flops=0, bytes_accessed=3_000_000 * microseconds, transcendentals=0
            ),
        )(*operands)

    return run


def local(les_wind, les_temp, acoustic_start):
    block = (LEVELS, COLS)
    groups = lax.axis_size("gy")
    (packed,) = call(
        strip_kernel,
        [(groups, 2, 2) + block],
        scratch=[les_wind.shape, les_temp.shape, (groups, 2, 2) + block],
        fetched=(0, 1),
        sent=True,
        semaphores=4,
        limit=PACK_LIMIT,
    )(les_wind, les_temp)
    tile, x_near, x_far, y_near, y_far = call(
        tile_kernel, [(3, ROWS) + block] + 2 * [(3, REACH) + block] + 2 * [(3, SIDE) + block]
    )(acoustic_start.reshape(3 * LEVELS * ROWS, COLS))
    coarse = lax.all_to_all(packed, "gy", split_axis=0, concat_axis=0, tiled=True)
    coarse = coarse.reshape((CROWS, 2) + block)
    x_near, x_far = swap_near(x_near, "gx"), swap_far(x_far, "gx")
    y_near, y_far = swap_near(y_near, "gy"), swap_far(y_far, "gy")
    s_near, s_far = call(second_pack_kernel, 2 * [(2 * HROWS + 3 * CREGS,) + block])(
        coarse, y_near, y_far
    )
    s_near, s_far = swap_near(s_near, "gx"), swap_far(s_far, "gx")
    edges, inside, refined = call(
        inner_kernel,
        [(STAGES, 2, 3, 2 * HAND) + block, (3, ROWS - 2 * REACH) + block, (2, 3, CROWS) + block],
        scratch=4 * [(2, 3, ROWS) + block] + [(3, ROWS) + block],
        microseconds=6,
    )(coarse, tile, y_near, y_far)
    scratch = [(2, 3, MARGIN + HROWS) + block, (2, 3, 2 * (MARGIN + HROWS)) + block]
    scratch += 3 * [(2, 3, REACH + REACH + HAND) + block]
    whole = (3 * LEVELS, ROWS, COLS)
    (near,) = call(
        near_end_kernel,
        [whole],
        scratch=scratch + [(3 * LEVELS * ROWS, COLS)],
        microseconds=3,
        sent=True,
        semaphores=1,
    )(x_near, s_near, edges, refined, inside)
    (end,) = call(
        far_end_kernel,
        [whole],
        scratch=scratch + [(3 * LEVELS * OWN, COLS)],
        microseconds=3,
        fetched=(5,),
        sent=True,
        semaphores=3,
        aliases={5: 0},
    )(x_far, s_far, edges, refined, inside, near)
    return end.reshape(acoustic_start.shape)


def solution(mesh):
    in_specs = (
        P(None, None, ("gx", "gy"), None),
        P(None, ("gx", "gy"), None),
        P(None, None, "gx", "gy"),
    )
    out_specs = P(None, None, "gx", "gy")
    return jax.shard_map(local, mesh=mesh, in_specs=in_specs, out_specs=out_specs, check_vma=False)
```

```python
import jax
import jax.numpy as jnp
from jax import lax
from jax.experimental import pallas as pl
from jax.experimental.pallas import tpu as pltpu
from jax.sharding import PartitionSpec as P

STEPS = 3
STAGES = 3 * STEPS
REACH = 2 * STAGES
LEVELS = 8
ROWS = 64
COLS = 128
EXT = ROWS + 2 * REACH
MARGIN = REACH // 2 + 1
CROWS = ROWS // 2
WINDOW = COLS // 2 + 2 * MARGIN
HALF = WINDOW // 2
RIGHT = 3 * REACH
RIM = 6 * REACH
EDGE = REACH // 3
MIDDLE = (ROWS - 2 * REACH) // 7
HROWS = REACH // 2
PAIRS = REACH // 2
PER = COLS // REACH
CREGS = -(-2 * PAIRS // PER)
OWN = -(-REACH // 8) * 8
HAND = 6
CHUNK = 16
PACK_LIMIT = 57
SIDE = EDGE + MIDDLE

time_step = 0.4
scale = time_step / 12.0

F32 = jnp.float32


def lanes():
    return lax.broadcasted_iota(jnp.int32, (LEVELS, COLS), 1)


def parity(axis):
    return lax.rem(lax.axis_index(axis), 2)


def swap_near(values, axis):
    return lax.ppermute(values, axis, [(i, i ^ 1) for i in range(lax.axis_size(axis))])


def swap_far(values, axis):
    count = lax.axis_size(axis)
    return lax.ppermute(
        values, axis, [(i, (i + 1) % count if i % 2 else (i - 1) % count) for i in range(count)]
    )


def roll(values, shift):
    if isinstance(shift, int):
        shift = shift % COLS
        if shift == 0:
            return values
    return pltpu.roll(values, shift, values.ndim - 1)


def slots():
    pieces = []
    for k in range(3):
        pieces.append((EDGE * k, EDGE, 0, k))
        pieces.append((ROWS - REACH + EDGE * k, EDGE, 0, 3 + k))
    for k in range(7):
        pieces.append((REACH + MIDDLE * k, MIDDLE, EDGE, k))
    return pieces


def pack_coarse(wind_ref, temp_ref, out_ref, sent):
    lane = lanes()
    blocks = wind_ref.shape[-1] // COLS

    def windows(values):
        parts = [values[:, COLS * i : COLS * (i + 1)] for i in range(blocks)]
        near = [roll(part, MARGIN) for part in parts]
        far = [roll(part, COLS // 2 + MARGIN) for part in parts]
        result = []
        for i in range(blocks):
            result.append(jnp.where(lane < MARGIN, near[i - 1], near[i]))
            result.append(jnp.where(lane < COLS // 2 + MARGIN, far[i], far[(i + 1) % blocks]))
        return result

    for row in range(2):
        east = windows(wind_ref[0, :, row, :])
        north = windows(wind_ref[1, :, row, :])
        warm = windows(temp_ref[:, row, :])
        for j in range(2 * blocks):
            out_ref[j, row, 0] = jnp.where(lane < WINDOW, east[j], roll(warm[j], WINDOW))
            out_ref[j, row, 1] = jnp.where(lane < WINDOW, north[j], roll(warm[j], HALF))
        sent[row].start()


def strip_kernel(wind_hbm, temp_hbm, packed_hbm, wind_ref, temp_ref, packed_ref, sems):
    wind_copy = pltpu.make_async_copy(wind_hbm, wind_ref, sems.at[0])
    temp_copy = pltpu.make_async_copy(temp_hbm, temp_ref, sems.at[1])
    wind_copy.start()
    temp_copy.start()
    sent = [
        pltpu.make_async_copy(packed_ref.at[:, row], packed_hbm.at[:, row], sems.at[2 + row])
        for row in range(2)
    ]
    wind_copy.wait()
    temp_copy.wait()
    pack_coarse(wind_ref, temp_ref, packed_ref, sent)
    sent[0].wait()
    sent[1].wait()


def tile_kernel(start_ref, tile_ref, x_near_ref, x_far_ref, y_near_ref, y_far_ref):
    x_odd, y_odd = parity("gx"), parity("gy")
    for f in range(3):
        for row in range(ROWS):
            values = start_ref[pl.ds(f * LEVELS * ROWS + row, LEVELS, stride=ROWS), :]
            tile_ref[f, row] = values * (1.0 / scale) if f == 0 else values
    x_near_ref[...] = tile_ref[:, pl.ds((1 - x_odd) * (ROWS - REACH), REACH)]
    x_far_ref[...] = tile_ref[:, pl.ds(x_odd * (ROWS - REACH), REACH)]
    lane = lanes()
    for ref, first in (
        (y_near_ref, (1 - y_odd) * (COLS - REACH)),
        (y_far_ref, y_odd * (COLS - REACH)),
    ):
        for f in range(3):
            for size, base in ((EDGE, 0), (MIDDLE, EDGE)):
                packed = None
                for row, count, register, slot in slots():
                    if register != base:
                        continue
                    shift = lax.rem(REACH * slot - first + COLS, COLS)
                    moved = roll(tile_ref[f, row : row + count], shift)
                    if packed is None:
                        packed = moved
                    else:
                        inside = (lane >= REACH * slot) & (lane < REACH * (slot + 1))
                        packed = jnp.where(inside, moved, packed)
                ref[f, base : base + size] = packed


def corner_slot(away, right):
    pair = min(away, REACH - 2 - away)
    register, slot = divmod(pair + PAIRS * right, PER)
    offset = 0
    if away > pair:
        offset = (REACH - 1 - pair) * (1 if right else -1)
    return register, REACH * slot, offset


def corner_lanes(away, right, lane):
    _, first, _ = corner_slot(away, right)
    pair = min(away, REACH - 2 - away)
    if away == pair:
        low, high = (0, REACH - 1 - away) if right else (1 + away, REACH)
    else:
        low, high = (REACH - 1 - pair, REACH) if right else (0, pair + 1)
    return (lane >= first + low) & (lane < first + high)


def second_pack_kernel(coarse_ref, y_near_ref, y_far_ref, x_near_ref, x_far_ref):
    x_odd, y_odd = parity("gx"), parity("gy")
    lane = lanes()
    for ref, bottom in ((x_near_ref, 1 - x_odd), (x_far_ref, x_odd)):
        first = bottom * (CROWS - HROWS)
        for i in range(HROWS):
            for c in range(2):
                ref[2 * i + c] = coarse_ref[first + i, c]
        for f in range(3):
            packed = [None] * CREGS
            for away in range(REACH - 1):
                slot, t = divmod(away, EDGE)
                register = t + bottom * (EDGE - 1 - 2 * t)
                source = REACH * (slot + bottom * (5 - 2 * slot))
                for right in range(2):
                    target, start, offset = corner_slot(away, right)
                    take_far = y_odd if right else 1 - y_odd
                    near = y_near_ref[f, register]
                    far = y_far_ref[f, register]
                    halo = jnp.where(jnp.full_like(lane, take_far) == 1, far, near)
                    moved = roll(halo, lax.rem(start + offset - source + 3 * COLS, COLS))
                    if packed[target] is None:
                        packed[target] = moved
                    else:
                        inside = corner_lanes(away, right, lane)
                        packed[target] = jnp.where(inside, moved, packed[target])
            for target in range(CREGS):
                ref[2 * HROWS + CREGS * f + target] = packed[target]


def rim_of(main, left, right, lane):
    own = jnp.where(lane < RIGHT, roll(main, REACH), roll(main, RIGHT - (COLS - 2 * REACH)))
    own = jnp.where(lane < REACH, left, own)
    return jnp.where(lane >= RIM - REACH, right, own)


def products(blocks, table):
    counts = [block.shape[0] * LEVELS for block in blocks]
    values = jnp.concatenate(
        [block.reshape(count, COLS) for block, count in zip(blocks, counts)], axis=0
    )
    high = values.astype(jnp.bfloat16)
    low = (values - high.astype(F32)).astype(jnp.bfloat16)
    result = jnp.dot(
        jnp.concatenate((high, low), axis=1),
        jnp.concatenate((table, table), axis=0),
        preferred_element_type=F32,
    )
    pieces, start = [], 0
    for count in counts:
        pieces.append(result[start : start + count])
        start += count
    return pieces


def stage_products(jobs, table):
    return products([rows[2:-2] for source, _, _, _ in jobs for rows in source], table)


def stage_sums(jobs, across, stage):
    for index, (source, base, background, store) in enumerate(jobs):
        mid = [rows[2:-2] for rows in source]
        count = mid[0].shape[0]
        dy = [across[3 * index + f].reshape(mid[0].shape) for f in range(3)]
        dx = [
            8.0 * (rows[3 : 3 + count] - rows[1 : 1 + count]) - (rows[4:] - rows[:count])
            for rows in source
        ]
        east, north, warm = background
        change = (
            east * dx[0] + north * dy[0] + (dx[1] + dy[2]),
            east * dx[1] + north * dy[1] + warm * dx[0],
            east * dx[2] + north * dy[2] + warm * dy[0],
        )
        for f in range(3):
            moved = mid[f] - change[f]
            if stage == 0:
                moved = (1.0 / 6.0) * moved
            elif stage == 1:
                moved = 0.5 * base[f] + moved
            else:
                moved = (1.0 / 3.0) * base[f] + moved
            store(f, moved)


def refine_columns(values, east_table, north_table, store):
    n = values.shape[0]
    (first,) = products([values[:, 0]], east_table)
    (second,) = products([values[:, 1]], north_table)
    warm = first[:, 2 * COLS :] + second[:, 2 * COLS :]
    for k in range(2):
        cut = slice(COLS * k, COLS * (k + 1))
        for f, result in enumerate((first, second, warm)):
            store(k, f, result[:, cut].reshape(n, LEVELS, COLS))


def merged(f, main, rim, lane):
    value = jnp.where(lane < REACH, roll(rim, -REACH), main)
    value = jnp.where(lane >= COLS - REACH, roll(rim, COLS - 2 * REACH - RIGHT), value)
    return value * scale if f == 0 else value


def inner_kernel(
    coarse_ref, tile_ref, y_near_ref, y_far_ref, edges_ref, inside_ref, refined_ref,
    east_ref, north_ref, table_ref, background, state, first, second, rim_ref,
):
    y_odd = parity("gy")
    lane = lanes()
    east_table, north_table, table = refine_table(0), refine_table(1), difference_table()
    east_ref[...], north_ref[...], table_ref[...] = east_table, north_table, table

    for start in range(0, CROWS, CHUNK):

        def keep(k, f, values, start=start):
            refined_ref[k, f, start : start + CHUNK] = values

        refine_columns(coarse_ref[start : start + CHUNK], east_table, north_table, keep)
    for k in range(2):
        for f in range(3):
            refine_rows(refined_ref, k, f, 0, CROWS, background, 0)

    take_near = (lane >= RIGHT).astype(jnp.int32) == 1 - y_odd
    for row, count, register, slot in slots():
        near_shift = lax.rem((1 - y_odd) * (RIM - REACH) - REACH * slot + COLS, COLS)
        far_shift = lax.rem(y_odd * (RIM - REACH) - REACH * slot + COLS, COLS)
        for f in range(3):
            near = roll(y_near_ref[f, register : register + count], near_shift)
            far = roll(y_far_ref[f, register : register + count], far_shift)
            halo = jnp.where(take_near, near, far)
            rim_ref[f, row : row + count] = rim_of(tile_ref[f, row : row + count], halo, halo, lane)

    class Start:
        def __getitem__(self, index):
            c, f, rows = index
            return (rim_ref if c else tile_ref)[f, rows]

    start_state = Start()
    for s in range(STAGES):
        origin = start_state if s < 3 else state
        buffers = (origin, first, second, state)
        source, target = buffers[s % 3], buffers[s % 3 + 1]
        for c in range(2):
            for f in range(3):
                edges_ref[s, c, f, :HAND] = source[c, f, 2 * s : 2 * s + HAND]
                edges_ref[s, c, f, HAND:] = source[c, f, ROWS - 2 * s - HAND : ROWS - 2 * s]
        low, top = 2 * (s + 1), ROWS - 2 * (s + 1)
        for start in range(low, top, CHUNK):
            stop = min(start + CHUNK, top)
            jobs = []
            for c in range(2):

                def store(f, values, c=c):
                    target[c, f, start:stop] = values

                jobs.append((
                    [source[c, f, start - 2 : stop + 2] for f in range(3)],
                    [origin[c, f, start:stop] for f in range(3)],
                    [background[c, f, start:stop] for f in range(3)],
                    store,
                ))
            stage_sums(jobs, stage_products(jobs, table), s % 3)
    for f in range(3):
        rows = slice(REACH, ROWS - REACH)
        inside_ref[f] = merged(f, state[0, f, rows], state[1, f, rows], lane)


def refine_rows(refined, k, f, start, count, background, first):
    block = refined[k, f, start : start + count]
    factor = scale * scale if f == 2 else scale
    centre = (0.75 * factor) * block
    side = (0.25 * factor) * block
    odd = centre[:-1] + side[1:]
    even = centre[1:] + side[:-1]
    for i in range(count - 1):
        background[k, f, first + 2 * i + 1] = odd[i]
        background[k, f, first + 2 * i + 2] = even[i]


def outer_end(
    side, main_ref, message_ref, edges_ref, refined_ref, tables, refined, background, state, first, second
):
    lane = lanes()
    east_table, north_table, table = (ref[...] for ref in tables)
    own = MARGIN + HROWS
    for k in range(2):
        for f in range(3):
            refined[k, f, pl.ds((1 - side) * HROWS, MARGIN)] = refined_ref[
                k, f, pl.ds(side * (CROWS - MARGIN), MARGIN)
            ]

    def keep(k, f, values):
        refined[k, f, pl.ds(side * MARGIN, HROWS)] = values[:HROWS]

    values = message_ref[: 2 * HROWS + 2].reshape(HROWS + 1, 2, LEVELS, COLS)
    refine_columns(values, east_table, north_table, keep)
    for k in range(2):
        for f in range(3):
            refine_rows(refined, k, f, 0, own, background, 0)

    halo = side * (REACH + HAND)
    for f in range(3):
        state[0, f, pl.ds(halo, REACH)] = main_ref[f]
        for away in range(REACH):
            row = REACH - 1 - away + side * (2 * away - REACH + 1)
            sides = []
            for right in range(2):
                register, start, offset = corner_slot(min(away, REACH - 2), right)
                corner = message_ref[2 * HROWS + CREGS * f + register]
                sides.append(roll(corner, (RIM - REACH) * right - start - offset))
            state[1, f, halo + row] = rim_of(main_ref[f, row], sides[0], sides[1], lane)

    buffers = (state, first, second, state)

    def job_of(c, s):
        source, target = buffers[s % 3], buffers[s % 3 + 1]
        low = 2 * (s + 1) + side * (REACH + 2 - 4 * s)
        handed = REACH + 2 * s - side * 4 * s
        for f in range(3):
            source[c, f, pl.ds(handed, HAND)] = edges_ref[s, c, f, pl.ds(side * HAND, HAND)]

        def store(f, values):
            target[c, f, pl.ds(low, REACH)] = values

        return (
            [source[c, f, pl.ds(low - 2, REACH + 4)] for f in range(3)],
            [state[c, f, pl.ds(low, REACH)] for f in range(3)],
            [background[c, f, pl.ds(low - 4 * side, REACH)] for f in range(3)],
            store,
        )

    waiting = [None, None]
    for s in range(STAGES + 1):
        for c in range(2):
            if waiting[c] is not None:
                stage_sums(waiting[c][0], waiting[c][1], (s - 1) % 3)
            if s < STAGES:
                jobs = [job_of(c, s)]
                waiting[c] = (jobs, stage_products(jobs, table))
    rows = pl.ds(REACH - 2 * HAND * side, REACH)
    return [merged(f, state[0, f, rows], state[1, f, rows], lane) for f in range(3)]


def place(out_ref, f, row, value):
    rows = out_ref.shape[0] // (3 * LEVELS)
    out_ref[pl.ds(f * LEVELS * rows + row, LEVELS, stride=rows), :] = value


def near_end_kernel(
    main_ref, message_ref, edges_ref, refined_ref, inside_ref, east_ref, north_ref, table_ref, end_ref,
    refined, background, state, first, second, out_ref, sem,
):
    side = 1 - parity("gx")
    for f in range(3):
        for row in range(ROWS - 2 * REACH):
            place(out_ref, f, REACH + row, inside_ref[f, row])
    ends = outer_end(
        side, main_ref, message_ref, edges_ref, refined_ref, (east_ref, north_ref, table_ref),
        refined, background, state, first, second,
    )
    for f in range(3):
        for row in range(REACH):
            place(out_ref, f, row + side * (ROWS - REACH), ends[f][row])
    source = out_ref.reshape(3 * LEVELS, ROWS, COLS)
    rows = pl.ds(pl.multiple_of(side * OWN, 8), ROWS - OWN)
    copy = pltpu.make_async_copy(source.at[:, rows], end_ref.at[:, rows], sem.at[0])
    copy.start()
    copy.wait()


def far_end_kernel(
    main_ref, message_ref, edges_ref, refined_ref, inside_ref, east_ref, north_ref, table_ref,
    before_ref, end_ref,
    refined, background, state, first, second, out_ref, sems,
):
    del before_ref
    side = parity("gx")
    spare = OWN - REACH
    for f in range(3):
        for row in range(spare):
            inner = row + side * (ROWS - 2 * REACH - spare)
            place(out_ref, f, row + (1 - side) * REACH, inside_ref[f, inner])
    ends = outer_end(
        side, main_ref, message_ref, edges_ref, refined_ref, (east_ref, north_ref, table_ref),
        refined, background, state, first, second,
    )
    target = out_ref.reshape(3 * LEVELS, OWN, COLS)
    rows = pl.ds(pl.multiple_of(side * (ROWS - OWN), 8), OWN)
    copies = []
    for f in range(3):
        for row in range(REACH):
            place(out_ref, f, row + side * spare, ends[f][row])
        field = pl.ds(f * LEVELS, LEVELS)
        copies.append(
            pltpu.make_async_copy(target.at[field], end_ref.at[field, rows], sems.at[f])
        )
        copies[f].start()
    for copy in copies:
        copy.wait()


def refine_table(north):
    row = lax.broadcasted_iota(jnp.int32, (COLS, 2 * COLS), 0)
    lane = lax.broadcasted_iota(jnp.int32, (COLS, 2 * COLS), 1)
    rim = lane - COLS
    column = jnp.where(rim < RIGHT, rim - REACH, rim - RIGHT + COLS - 2 * REACH)
    column = jnp.where(lane < COLS, lane, column)
    centre = lax.shift_right_arithmetic(column, 1) + MARGIN
    side = centre - 1 + 2 * (column & 1)

    def weights(window, used):
        weight = jnp.where(window == centre, 0.75, jnp.where(window == side, 0.25, 0.0))
        return jnp.where(used & (rim < RIM), weight, 0.0).astype(jnp.bfloat16)

    wind = weights(row, row < WINDOW)
    warm = weights(row - WINDOW + HALF * north, (row >= WINDOW) & (row < WINDOW + HALF))
    return jnp.concatenate((wind, warm), axis=1)


def difference_table():
    source = lax.broadcasted_iota(jnp.int32, (COLS, COLS), 0)
    lane = lax.broadcasted_iota(jnp.int32, (COLS, COLS), 1)
    ahead = (source - lane) & (COLS - 1)
    table = jnp.where(ahead == 1, 8.0, 0.0) - jnp.where(ahead == COLS - 1, 8.0, 0.0)
    table = table - jnp.where(ahead == 2, 1.0, 0.0) + jnp.where(ahead == COLS - 2, 1.0, 0.0)
    return table.astype(jnp.bfloat16)


def call(
    kernel, outputs, scratch=(), limit=48, microseconds=1, fetched=(), sent=False, semaphores=0,
    aliases=None,
):
    here, there = pl.BlockSpec(memory_space=pltpu.VMEM), pl.BlockSpec(memory_space=pltpu.HBM)

    def run(*operands):
        return pl.pallas_call(
            kernel,
            out_shape=[
                jax.ShapeDtypeStruct(shape, F32) if isinstance(shape, tuple) else shape
                for shape in outputs
            ],
            in_specs=[there if i in fetched else here for i in range(len(operands))],
            out_specs=[there if sent else here] * len(outputs),
            scratch_shapes=[pltpu.VMEM(shape, F32) for shape in scratch]
            + ([pltpu.SemaphoreType.DMA((semaphores,))] if semaphores else []),
            input_output_aliases=aliases or {},
            compiler_params=pltpu.CompilerParams(vmem_limit_bytes=limit * 2**20),
            cost_estimate=pl.CostEstimate(
                flops=0, bytes_accessed=3_000_000 * microseconds, transcendentals=0
            ),
        )(*operands)

    return run


def local(les_wind, les_temp, acoustic_start):
    block = (LEVELS, COLS)
    groups = lax.axis_size("gy")
    (packed,) = call(
        strip_kernel,
        [(groups, 2, 2) + block],
        scratch=[les_wind.shape, les_temp.shape, (groups, 2, 2) + block],
        fetched=(0, 1),
        sent=True,
        semaphores=4,
        limit=PACK_LIMIT,
    )(les_wind, les_temp)
    tile, x_near, x_far, y_near, y_far = call(
        tile_kernel, [(3, ROWS) + block] + 2 * [(3, REACH) + block] + 2 * [(3, SIDE) + block]
    )(acoustic_start.reshape(3 * LEVELS * ROWS, COLS))
    coarse = lax.all_to_all(packed, "gy", split_axis=0, concat_axis=0, tiled=True)
    coarse = coarse.reshape((CROWS, 2) + block)
    x_near, x_far = swap_near(x_near, "gx"), swap_far(x_far, "gx")
    y_near, y_far = swap_near(y_near, "gy"), swap_far(y_far, "gy")
    s_near, s_far = call(second_pack_kernel, 2 * [(2 * HROWS + 3 * CREGS,) + block])(
        coarse, y_near, y_far
    )
    s_near, s_far = swap_near(s_near, "gx"), swap_far(s_far, "gx")
    edges, inside, refined, *made = call(
        inner_kernel,
        [(STAGES, 2, 3, 2 * HAND) + block, (3, ROWS - 2 * REACH) + block, (2, 3, CROWS) + block]
        + [jax.ShapeDtypeStruct((COLS, n * COLS), jnp.bfloat16) for n in (4, 4, 1)],
        scratch=4 * [(2, 3, ROWS) + block] + [(3, ROWS) + block],
        microseconds=6,
    )(coarse, tile, y_near, y_far)
    scratch = [(2, 3, MARGIN + HROWS) + block, (2, 3, 2 * (MARGIN + HROWS)) + block]
    scratch += 3 * [(2, 3, REACH + REACH + HAND) + block]
    whole = (3 * LEVELS, ROWS, COLS)
    (near,) = call(
        near_end_kernel,
        [whole],
        scratch=scratch + [(3 * LEVELS * ROWS, COLS)],
        microseconds=3,
        sent=True,
        semaphores=1,
    )(x_near, s_near, edges, refined, inside, *made)
    (end,) = call(
        far_end_kernel,
        [whole],
        scratch=scratch + [(3 * LEVELS * OWN, COLS)],
        microseconds=3,
        fetched=(8,),
        sent=True,
        semaphores=3,
        aliases={8: 0},
    )(x_far, s_far, edges, refined, inside, *made, near)
    return end.reshape(acoustic_start.shape)


def solution(mesh):
    in_specs = (
        P(None, None, ("gx", "gy"), None),
        P(None, ("gx", "gy"), None),
        P(None, None, "gx", "gy"),
    )
    out_specs = P(None, None, "gx", "gy")
    return jax.shard_map(local, mesh=mesh, in_specs=in_specs, out_specs=out_specs, check_vma=False)
```

```python
import jax
import jax.numpy as jnp
from jax import lax
from jax.experimental import pallas as pl
from jax.experimental.pallas import tpu as pltpu
from jax.sharding import PartitionSpec as P

STEPS = 3
STAGES = 3 * STEPS
REACH = 2 * STAGES
LEVELS = 8
ROWS = 64
COLS = 128
EXT = ROWS + 2 * REACH
MARGIN = REACH // 2 + 1
CROWS = ROWS // 2
WINDOW = COLS // 2 + 2 * MARGIN
HALF = WINDOW // 2
RIGHT = 3 * REACH
RIM = 6 * REACH
EDGE = REACH // 3
MIDDLE = (ROWS - 2 * REACH) // 7
HROWS = REACH // 2
PAIRS = REACH // 2
PER = COLS // REACH
CREGS = -(-2 * PAIRS // PER)
OWN = -(-REACH // 8) * 8
HAND = 6
CHUNK = 16
PACK_LIMIT = 57
SIDE = EDGE + MIDDLE

time_step = 0.4
scale = time_step / 12.0

F32 = jnp.float32


def lanes():
    return lax.broadcasted_iota(jnp.int32, (LEVELS, COLS), 1)


def parity(axis):
    return lax.rem(lax.axis_index(axis), 2)


def swap_near(values, axis):
    return lax.ppermute(values, axis, [(i, i ^ 1) for i in range(lax.axis_size(axis))])


def swap_far(values, axis):
    count = lax.axis_size(axis)
    return lax.ppermute(
        values, axis, [(i, (i + 1) % count if i % 2 else (i - 1) % count) for i in range(count)]
    )


def roll(values, shift):
    if isinstance(shift, int):
        shift = shift % COLS
        if shift == 0:
            return values
    return pltpu.roll(values, shift, values.ndim - 1)


def slots():
    pieces = []
    for k in range(3):
        pieces.append((EDGE * k, EDGE, 0, k))
        pieces.append((ROWS - REACH + EDGE * k, EDGE, 0, 3 + k))
    for k in range(7):
        pieces.append((REACH + MIDDLE * k, MIDDLE, EDGE, k))
    return pieces


def pack_coarse(wind_ref, temp_ref, out_ref, sent):
    lane = lanes()
    blocks = wind_ref.shape[-1] // COLS

    def windows(values):
        parts = [values[:, COLS * i : COLS * (i + 1)] for i in range(blocks)]
        near = [roll(part, MARGIN) for part in parts]
        far = [roll(part, COLS // 2 + MARGIN) for part in parts]
        result = []
        for i in range(blocks):
            result.append(jnp.where(lane < MARGIN, near[i - 1], near[i]))
            result.append(jnp.where(lane < COLS // 2 + MARGIN, far[i], far[(i + 1) % blocks]))
        return result

    for row in range(2):
        east = windows(wind_ref[0, :, row, :])
        north = windows(wind_ref[1, :, row, :])
        warm = windows(temp_ref[:, row, :])
        for j in range(2 * blocks):
            out_ref[j, row, 0] = jnp.where(lane < WINDOW, east[j], roll(warm[j], WINDOW))
            out_ref[j, row, 1] = jnp.where(lane < WINDOW, north[j], roll(warm[j], HALF))
        sent[row].start()


def strip_kernel(wind_hbm, temp_hbm, packed_hbm, wind_ref, temp_ref, packed_ref, sems):
    wind_copy = pltpu.make_async_copy(wind_hbm, wind_ref, sems.at[0])
    temp_copy = pltpu.make_async_copy(temp_hbm, temp_ref, sems.at[1])
    wind_copy.start()
    temp_copy.start()
    sent = [
        pltpu.make_async_copy(packed_ref.at[:, row], packed_hbm.at[:, row], sems.at[2 + row])
        for row in range(2)
    ]
    wind_copy.wait()
    temp_copy.wait()
    pack_coarse(wind_ref, temp_ref, packed_ref, sent)
    sent[0].wait()
    sent[1].wait()


def tile_kernel(start_ref, tile_ref, x_near_ref, x_far_ref, y_near_ref, y_far_ref):
    x_odd, y_odd = parity("gx"), parity("gy")
    for f in range(3):
        for row in range(ROWS):
            values = start_ref[pl.ds(f * LEVELS * ROWS + row, LEVELS, stride=ROWS), :]
            tile_ref[f, row] = values * (1.0 / scale) if f == 0 else values
    x_near_ref[...] = tile_ref[:, pl.ds((1 - x_odd) * (ROWS - REACH), REACH)]
    x_far_ref[...] = tile_ref[:, pl.ds(x_odd * (ROWS - REACH), REACH)]
    lane = lanes()
    for ref, first in (
        (y_near_ref, (1 - y_odd) * (COLS - REACH)),
        (y_far_ref, y_odd * (COLS - REACH)),
    ):
        for f in range(3):
            for size, base in ((EDGE, 0), (MIDDLE, EDGE)):
                packed = None
                for row, count, register, slot in slots():
                    if register != base:
                        continue
                    shift = lax.rem(REACH * slot - first + COLS, COLS)
                    moved = roll(tile_ref[f, row : row + count], shift)
                    if packed is None:
                        packed = moved
                    else:
                        inside = (lane >= REACH * slot) & (lane < REACH * (slot + 1))
                        packed = jnp.where(inside, moved, packed)
                ref[f, base : base + size] = packed


def corner_slot(away, right):
    pair = min(away, REACH - 2 - away)
    register, slot = divmod(pair + PAIRS * right, PER)
    offset = 0
    if away > pair:
        offset = (REACH - 1 - pair) * (1 if right else -1)
    return register, REACH * slot, offset


def corner_lanes(away, right, lane):
    _, first, _ = corner_slot(away, right)
    pair = min(away, REACH - 2 - away)
    if away == pair:
        low, high = (0, REACH - 1 - away) if right else (1 + away, REACH)
    else:
        low, high = (REACH - 1 - pair, REACH) if right else (0, pair + 1)
    return (lane >= first + low) & (lane < first + high)


def second_pack_kernel(coarse_ref, y_near_ref, y_far_ref, x_near_ref, x_far_ref):
    x_odd, y_odd = parity("gx"), parity("gy")
    lane = lanes()
    for ref, bottom in ((x_near_ref, 1 - x_odd), (x_far_ref, x_odd)):
        first = bottom * (CROWS - HROWS)
        for i in range(HROWS):
            for c in range(2):
                ref[2 * i + c] = coarse_ref[first + i, c]
        for f in range(3):
            packed = [None] * CREGS
            for away in range(REACH - 1):
                slot, t = divmod(away, EDGE)
                register = t + bottom * (EDGE - 1 - 2 * t)
                source = REACH * (slot + bottom * (5 - 2 * slot))
                for right in range(2):
                    target, start, offset = corner_slot(away, right)
                    take_far = y_odd if right else 1 - y_odd
                    near = y_near_ref[f, register]
                    far = y_far_ref[f, register]
                    halo = jnp.where(jnp.full_like(lane, take_far) == 1, far, near)
                    moved = roll(halo, lax.rem(start + offset - source + 3 * COLS, COLS))
                    if packed[target] is None:
                        packed[target] = moved
                    else:
                        inside = corner_lanes(away, right, lane)
                        packed[target] = jnp.where(inside, moved, packed[target])
            for target in range(CREGS):
                ref[2 * HROWS + CREGS * f + target] = packed[target]


def rim_of(main, left, right, lane):
    own = jnp.where(lane < RIGHT, roll(main, REACH), roll(main, RIGHT - (COLS - 2 * REACH)))
    own = jnp.where(lane < REACH, left, own)
    return jnp.where(lane >= RIM - REACH, right, own)


def products(blocks, table):
    counts = [block.shape[0] * LEVELS for block in blocks]
    values = jnp.concatenate(
        [block.reshape(count, COLS) for block, count in zip(blocks, counts)], axis=0
    )
    high = values.astype(jnp.bfloat16)
    low = (values - high.astype(F32)).astype(jnp.bfloat16)
    result = jnp.dot(
        jnp.concatenate((high, low), axis=1),
        jnp.concatenate((table, table), axis=0),
        preferred_element_type=F32,
    )
    pieces, start = [], 0
    for count in counts:
        pieces.append(result[start : start + count])
        start += count
    return pieces


def stage_products(jobs, table):
    return products([rows[2:-2] for source, _, _, _ in jobs for rows in source], table)


def stage_sums(jobs, across, stage):
    for index, (source, base, background, store) in enumerate(jobs):
        mid = [rows[2:-2] for rows in source]
        count = mid[0].shape[0]
        dy = [across[3 * index + f].reshape(mid[0].shape) for f in range(3)]
        dx = [
            8.0 * (rows[3 : 3 + count] - rows[1 : 1 + count]) - (rows[4:] - rows[:count])
            for rows in source
        ]
        east, north, warm = background
        change = (
            east * dx[0] + north * dy[0] + (dx[1] + dy[2]),
            east * dx[1] + north * dy[1] + warm * dx[0],
            east * dx[2] + north * dy[2] + warm * dy[0],
        )
        for f in range(3):
            moved = mid[f] - change[f]
            if stage == 0:
                moved = (1.0 / 6.0) * moved
            elif stage == 1:
                moved = 0.5 * base[f] + moved
            else:
                moved = (1.0 / 3.0) * base[f] + moved
            store(f, moved)


def refine_columns(values, east_table, north_table, store):
    n = values.shape[0]
    (first,) = products([values[:, 0]], east_table)
    (second,) = products([values[:, 1]], north_table)
    warm = first[:, 2 * COLS :] + second[:, 2 * COLS :]
    for k in range(2):
        cut = slice(COLS * k, COLS * (k + 1))
        for f, result in enumerate((first, second, warm)):
            store(k, f, result[:, cut].reshape(n, LEVELS, COLS))


def merged(f, main, rim, lane):
    value = jnp.where(lane < REACH, roll(rim, -REACH), main)
    value = jnp.where(lane >= COLS - REACH, roll(rim, COLS - 2 * REACH - RIGHT), value)
    return value * scale if f == 0 else value


def inner_kernel(
    coarse_ref, tile_ref, y_near_ref, y_far_ref, edges_ref, inside_ref, refined_ref,
    background, state, first, second, rim_ref,
):
    y_odd = parity("gy")
    lane = lanes()
    east_table, north_table, table = refine_table(0), refine_table(1), difference_table()

    for start in range(0, CROWS, CHUNK):

        def keep(k, f, values, start=start):
            refined_ref[k, f, start : start + CHUNK] = values

        refine_columns(coarse_ref[start : start + CHUNK], east_table, north_table, keep)
    for k in range(2):
        for f in range(3):
            refine_rows(refined_ref, k, f, 0, CROWS, background, 0)

    take_near = (lane >= RIGHT).astype(jnp.int32) == 1 - y_odd
    for row, count, register, slot in slots():
        near_shift = lax.rem((1 - y_odd) * (RIM - REACH) - REACH * slot + COLS, COLS)
        far_shift = lax.rem(y_odd * (RIM - REACH) - REACH * slot + COLS, COLS)
        for f in range(3):
            near = roll(y_near_ref[f, register : register + count], near_shift)
            far = roll(y_far_ref[f, register : register + count], far_shift)
            halo = jnp.where(take_near, near, far)
            rim_ref[f, row : row + count] = rim_of(tile_ref[f, row : row + count], halo, halo, lane)

    class Start:
        def __getitem__(self, index):
            c, f, rows = index
            return (rim_ref if c else tile_ref)[f, rows]

    start_state = Start()
    for s in range(STAGES):
        origin = start_state if s < 3 else state
        buffers = (origin, first, second, state)
        source, target = buffers[s % 3], buffers[s % 3 + 1]
        for c in range(2):
            for f in range(3):
                edges_ref[s, c, f, :HAND] = source[c, f, 2 * s : 2 * s + HAND]
                edges_ref[s, c, f, HAND:] = source[c, f, ROWS - 2 * s - HAND : ROWS - 2 * s]
        low, top = 2 * (s + 1), ROWS - 2 * (s + 1)
        for start in range(low, top, CHUNK):
            stop = min(start + CHUNK, top)
            jobs = []
            for c in range(2):

                def store(f, values, c=c):
                    target[c, f, start:stop] = values

                jobs.append((
                    [source[c, f, start - 2 : stop + 2] for f in range(3)],
                    [origin[c, f, start:stop] for f in range(3)],
                    [background[c, f, start:stop] for f in range(3)],
                    store,
                ))
            stage_sums(jobs, stage_products(jobs, table), s % 3)
    for f in range(3):
        rows = slice(REACH, ROWS - REACH)
        inside_ref[f] = merged(f, state[0, f, rows], state[1, f, rows], lane)


def refine_rows(refined, k, f, start, count, background, first):
    block = refined[k, f, start : start + count]
    factor = scale * scale if f == 2 else scale
    centre = (0.75 * factor) * block
    side = (0.25 * factor) * block
    odd = centre[:-1] + side[1:]
    even = centre[1:] + side[:-1]
    for i in range(count - 1):
        background[k, f, first + 2 * i + 1] = odd[i]
        background[k, f, first + 2 * i + 2] = even[i]


def outer_end(
    side, main_ref, message_ref, edges_ref, refined_ref, refined, background, state, first, second
):
    lane = lanes()
    halo = side * (REACH + HAND)
    for f in range(3):
        state[0, f, pl.ds(halo, REACH)] = main_ref[f]
        for away in range(REACH):
            row = REACH - 1 - away + side * (2 * away - REACH + 1)
            sides = []
            for right in range(2):
                register, start, offset = corner_slot(min(away, REACH - 2), right)
                corner = message_ref[2 * HROWS + CREGS * f + register]
                sides.append(roll(corner, (RIM - REACH) * right - start - offset))
            state[1, f, halo + row] = rim_of(main_ref[f, row], sides[0], sides[1], lane)

    east_table, north_table, table = refine_table(0), refine_table(1), difference_table()
    own = MARGIN + HROWS
    for k in range(2):
        for f in range(3):
            refined[k, f, pl.ds((1 - side) * HROWS, MARGIN)] = refined_ref[
                k, f, pl.ds(side * (CROWS - MARGIN), MARGIN)
            ]

    def keep(k, f, values):
        refined[k, f, pl.ds(side * MARGIN, HROWS)] = values[:HROWS]

    values = message_ref[: 2 * HROWS + 2].reshape(HROWS + 1, 2, LEVELS, COLS)
    refine_columns(values, east_table, north_table, keep)
    for k in range(2):
        for f in range(3):
            refine_rows(refined, k, f, 0, own, background, 0)

    buffers = (state, first, second, state)

    def job_of(c, s):
        source, target = buffers[s % 3], buffers[s % 3 + 1]
        low = 2 * (s + 1) + side * (REACH + 2 - 4 * s)
        handed = REACH + 2 * s - side * 4 * s
        for f in range(3):
            source[c, f, pl.ds(handed, HAND)] = edges_ref[s, c, f, pl.ds(side * HAND, HAND)]

        def store(f, values):
            target[c, f, pl.ds(low, REACH)] = values

        return (
            [source[c, f, pl.ds(low - 2, REACH + 4)] for f in range(3)],
            [state[c, f, pl.ds(low, REACH)] for f in range(3)],
            [background[c, f, pl.ds(low - 4 * side, REACH)] for f in range(3)],
            store,
        )

    waiting = [None, None]
    for s in range(STAGES + 1):
        for c in range(2):
            if waiting[c] is not None:
                stage_sums(waiting[c][0], waiting[c][1], (s - 1) % 3)
            if s < STAGES:
                jobs = [job_of(c, s)]
                waiting[c] = (jobs, stage_products(jobs, table))
    rows = pl.ds(REACH - 2 * HAND * side, REACH)
    return [merged(f, state[0, f, rows], state[1, f, rows], lane) for f in range(3)]


def place(out_ref, f, row, value):
    rows = out_ref.shape[0] // (3 * LEVELS)
    out_ref[pl.ds(f * LEVELS * rows + row, LEVELS, stride=rows), :] = value


def near_end_kernel(
    main_ref, message_ref, edges_ref, refined_ref, inside_ref, end_ref,
    refined, background, state, first, second, out_ref, sem,
):
    side = 1 - parity("gx")
    for f in range(3):
        for row in range(ROWS - 2 * REACH):
            place(out_ref, f, REACH + row, inside_ref[f, row])
    ends = outer_end(
        side, main_ref, message_ref, edges_ref, refined_ref, refined, background, state, first, second
    )
    for f in range(3):
        for row in range(REACH):
            place(out_ref, f, row + side * (ROWS - REACH), ends[f][row])
    source = out_ref.reshape(3 * LEVELS, ROWS, COLS)
    rows = pl.ds(pl.multiple_of(side * OWN, 8), ROWS - OWN)
    copy = pltpu.make_async_copy(source.at[:, rows], end_ref.at[:, rows], sem.at[0])
    copy.start()
    copy.wait()


def far_end_kernel(
    main_ref, message_ref, edges_ref, refined_ref, inside_ref, before_ref, end_ref,
    refined, background, state, first, second, out_ref, sems,
):
    del before_ref
    side = parity("gx")
    spare = OWN - REACH
    for f in range(3):
        for row in range(spare):
            inner = row + side * (ROWS - 2 * REACH - spare)
            place(out_ref, f, row + (1 - side) * REACH, inside_ref[f, inner])
    ends = outer_end(
        side, main_ref, message_ref, edges_ref, refined_ref, refined, background, state, first, second
    )
    target = out_ref.reshape(3 * LEVELS, OWN, COLS)
    rows = pl.ds(pl.multiple_of(side * (ROWS - OWN), 8), OWN)
    copies = []
    for f in range(3):
        for row in range(REACH):
            place(out_ref, f, row + side * spare, ends[f][row])
        field = pl.ds(f * LEVELS, LEVELS)
        copies.append(
            pltpu.make_async_copy(target.at[field], end_ref.at[field, rows], sems.at[f])
        )
        copies[f].start()
    for copy in copies:
        copy.wait()


def refine_table(north):
    row = lax.broadcasted_iota(jnp.int32, (COLS, 2 * COLS), 0)
    lane = lax.broadcasted_iota(jnp.int32, (COLS, 2 * COLS), 1)
    rim = lane - COLS
    column = jnp.where(rim < RIGHT, rim - REACH, rim - RIGHT + COLS - 2 * REACH)
    column = jnp.where(lane < COLS, lane, column)
    centre = lax.shift_right_arithmetic(column, 1) + MARGIN
    side = centre - 1 + 2 * (column & 1)

    def weights(window, used):
        weight = jnp.where(window == centre, 0.75, jnp.where(window == side, 0.25, 0.0))
        return jnp.where(used & (rim < RIM), weight, 0.0).astype(jnp.bfloat16)

    wind = weights(row, row < WINDOW)
    warm = weights(row - WINDOW + HALF * north, (row >= WINDOW) & (row < WINDOW + HALF))
    return jnp.concatenate((wind, warm), axis=1)


def difference_table():
    source = lax.broadcasted_iota(jnp.int32, (COLS, COLS), 0)
    lane = lax.broadcasted_iota(jnp.int32, (COLS, COLS), 1)
    ahead = (source - lane) & (COLS - 1)
    table = jnp.where(ahead == 1, 8.0, 0.0) - jnp.where(ahead == COLS - 1, 8.0, 0.0)
    table = table - jnp.where(ahead == 2, 1.0, 0.0) + jnp.where(ahead == COLS - 2, 1.0, 0.0)
    return table.astype(jnp.bfloat16)


def call(
    kernel, outputs, scratch=(), limit=48, microseconds=1, fetched=(), sent=False, semaphores=0,
    aliases=None,
):
    here, there = pl.BlockSpec(memory_space=pltpu.VMEM), pl.BlockSpec(memory_space=pltpu.HBM)

    def run(*operands):
        return pl.pallas_call(
            kernel,
            out_shape=[jax.ShapeDtypeStruct(shape, F32) for shape in outputs],
            in_specs=[there if i in fetched else here for i in range(len(operands))],
            out_specs=[there if sent else here] * len(outputs),
            scratch_shapes=[pltpu.VMEM(shape, F32) for shape in scratch]
            + ([pltpu.SemaphoreType.DMA((semaphores,))] if semaphores else []),
            input_output_aliases=aliases or {},
            compiler_params=pltpu.CompilerParams(vmem_limit_bytes=limit * 2**20),
            cost_estimate=pl.CostEstimate(
                flops=0, bytes_accessed=3_000_000 * microseconds, transcendentals=0
            ),
        )(*operands)

    return run


def local(les_wind, les_temp, acoustic_start):
    block = (LEVELS, COLS)
    groups = lax.axis_size("gy")
    (packed,) = call(
        strip_kernel,
        [(groups, 2, 2) + block],
        scratch=[les_wind.shape, les_temp.shape, (groups, 2, 2) + block],
        fetched=(0, 1),
        sent=True,
        semaphores=4,
        limit=PACK_LIMIT,
    )(les_wind, les_temp)
    tile, x_near, x_far, y_near, y_far = call(
        tile_kernel, [(3, ROWS) + block] + 2 * [(3, REACH) + block] + 2 * [(3, SIDE) + block]
    )(acoustic_start.reshape(3 * LEVELS * ROWS, COLS))
    coarse = lax.all_to_all(packed, "gy", split_axis=0, concat_axis=0, tiled=True)
    coarse = coarse.reshape((CROWS, 2) + block)
    x_near, x_far = swap_near(x_near, "gx"), swap_far(x_far, "gx")
    y_near, y_far = swap_near(y_near, "gy"), swap_far(y_far, "gy")
    s_near, s_far = call(second_pack_kernel, 2 * [(2 * HROWS + 3 * CREGS,) + block])(
        coarse, y_near, y_far
    )
    s_near, s_far = swap_near(s_near, "gx"), swap_far(s_far, "gx")
    edges, inside, refined = call(
        inner_kernel,
        [(STAGES, 2, 3, 2 * HAND) + block, (3, ROWS - 2 * REACH) + block, (2, 3, CROWS) + block],
        scratch=4 * [(2, 3, ROWS) + block] + [(3, ROWS) + block],
        microseconds=6,
    )(coarse, tile, y_near, y_far)
    scratch = [(2, 3, MARGIN + HROWS) + block, (2, 3, 2 * (MARGIN + HROWS)) + block]
    scratch += 3 * [(2, 3, REACH + REACH + HAND) + block]
    whole = (3 * LEVELS, ROWS, COLS)
    (near,) = call(
        near_end_kernel,
        [whole],
        scratch=scratch + [(3 * LEVELS * ROWS, COLS)],
        microseconds=3,
        sent=True,
        semaphores=1,
    )(x_near, s_near, edges, refined, inside)
    (end,) = call(
        far_end_kernel,
        [whole],
        scratch=scratch + [(3 * LEVELS * OWN, COLS)],
        microseconds=3,
        fetched=(5,),
        sent=True,
        semaphores=3,
        aliases={5: 0},
    )(x_far, s_far, edges, refined, inside, near)
    return end.reshape(acoustic_start.shape)


def solution(mesh):
    in_specs = (
        P(None, None, ("gx", "gy"), None),
        P(None, ("gx", "gy"), None),
        P(None, None, "gx", "gy"),
    )
    out_specs = P(None, None, "gx", "gy")
    return jax.shard_map(local, mesh=mesh, in_specs=in_specs, out_specs=out_specs, check_vma=False)
```

```python
import jax
import jax.numpy as jnp
from jax import lax
from jax.experimental import pallas as pl
from jax.experimental.pallas import tpu as pltpu
from jax.sharding import PartitionSpec as P

STEPS = 3
STAGES = 3 * STEPS
REACH = 2 * STAGES
LEVELS = 8
ROWS = 64
COLS = 128
EXT = ROWS + 2 * REACH
MARGIN = REACH // 2 + 1
CROWS = ROWS // 2
WINDOW = COLS // 2 + 2 * MARGIN
HALF = WINDOW // 2
RIGHT = 3 * REACH
RIM = 6 * REACH
EDGE = REACH // 3
MIDDLE = (ROWS - 2 * REACH) // 7
HROWS = REACH // 2
PAIRS = REACH // 2
PER = COLS // REACH
CREGS = -(-2 * PAIRS // PER)
OWN = -(-REACH // 8) * 8
HAND = 6
CHUNK = 8
PACK_LIMIT = 57
SIDE = EDGE + MIDDLE

time_step = 0.4
scale = time_step / 12.0

F32 = jnp.float32


def lanes():
    return lax.broadcasted_iota(jnp.int32, (LEVELS, COLS), 1)


def parity(axis):
    return lax.rem(lax.axis_index(axis), 2)


def swap_near(values, axis):
    return lax.ppermute(values, axis, [(i, i ^ 1) for i in range(lax.axis_size(axis))])


def swap_far(values, axis):
    count = lax.axis_size(axis)
    return lax.ppermute(
        values, axis, [(i, (i + 1) % count if i % 2 else (i - 1) % count) for i in range(count)]
    )


def roll(values, shift):
    if isinstance(shift, int):
        shift = shift % COLS
        if shift == 0:
            return values
    return pltpu.roll(values, shift, values.ndim - 1)


def slots():
    pieces = []
    for k in range(3):
        pieces.append((EDGE * k, EDGE, 0, k))
        pieces.append((ROWS - REACH + EDGE * k, EDGE, 0, 3 + k))
    for k in range(7):
        pieces.append((REACH + MIDDLE * k, MIDDLE, EDGE, k))
    return pieces


def pack_coarse(wind_ref, temp_ref, out_ref, sent):
    lane = lanes()
    blocks = wind_ref.shape[-1] // COLS

    def windows(values):
        parts = [values[:, COLS * i : COLS * (i + 1)] for i in range(blocks)]
        near = [roll(part, MARGIN) for part in parts]
        far = [roll(part, COLS // 2 + MARGIN) for part in parts]
        result = []
        for i in range(blocks):
            result.append(jnp.where(lane < MARGIN, near[i - 1], near[i]))
            result.append(jnp.where(lane < COLS // 2 + MARGIN, far[i], far[(i + 1) % blocks]))
        return result

    for row in range(2):
        east = windows(wind_ref[0, :, row, :])
        north = windows(wind_ref[1, :, row, :])
        warm = windows(temp_ref[:, row, :])
        for j in range(2 * blocks):
            out_ref[j, row, 0] = jnp.where(lane < WINDOW, east[j], roll(warm[j], WINDOW))
            out_ref[j, row, 1] = jnp.where(lane < WINDOW, north[j], roll(warm[j], HALF))
        sent[row].start()


def strip_kernel(wind_hbm, temp_hbm, packed_hbm, wind_ref, temp_ref, packed_ref, sems):
    wind_copy = pltpu.make_async_copy(wind_hbm, wind_ref, sems.at[0])
    temp_copy = pltpu.make_async_copy(temp_hbm, temp_ref, sems.at[1])
    wind_copy.start()
    temp_copy.start()
    sent = [
        pltpu.make_async_copy(packed_ref.at[:, row], packed_hbm.at[:, row], sems.at[2 + row])
        for row in range(2)
    ]
    wind_copy.wait()
    temp_copy.wait()
    pack_coarse(wind_ref, temp_ref, packed_ref, sent)
    sent[0].wait()
    sent[1].wait()


def tile_kernel(start_ref, tile_ref, x_near_ref, x_far_ref, y_near_ref, y_far_ref):
    x_odd, y_odd = parity("gx"), parity("gy")
    for f in range(3):
        for row in range(ROWS):
            values = start_ref[pl.ds(f * LEVELS * ROWS + row, LEVELS, stride=ROWS), :]
            tile_ref[f, row] = values * (1.0 / scale) if f == 0 else values
    x_near_ref[...] = tile_ref[:, pl.ds((1 - x_odd) * (ROWS - REACH), REACH)]
    x_far_ref[...] = tile_ref[:, pl.ds(x_odd * (ROWS - REACH), REACH)]
    lane = lanes()
    for ref, first in (
        (y_near_ref, (1 - y_odd) * (COLS - REACH)),
        (y_far_ref, y_odd * (COLS - REACH)),
    ):
        for f in range(3):
            for size, base in ((EDGE, 0), (MIDDLE, EDGE)):
                packed = None
                for row, count, register, slot in slots():
                    if register != base:
                        continue
                    shift = lax.rem(REACH * slot - first + COLS, COLS)
                    moved = roll(tile_ref[f, row : row + count], shift)
                    if packed is None:
                        packed = moved
                    else:
                        inside = (lane >= REACH * slot) & (lane < REACH * (slot + 1))
                        packed = jnp.where(inside, moved, packed)
                ref[f, base : base + size] = packed


def corner_slot(away, right):
    pair = min(away, REACH - 2 - away)
    register, slot = divmod(pair + PAIRS * right, PER)
    offset = 0
    if away > pair:
        offset = (REACH - 1 - pair) * (1 if right else -1)
    return register, REACH * slot, offset


def corner_lanes(away, right, lane):
    _, first, _ = corner_slot(away, right)
    pair = min(away, REACH - 2 - away)
    if away == pair:
        low, high = (0, REACH - 1 - away) if right else (1 + away, REACH)
    else:
        low, high = (REACH - 1 - pair, REACH) if right else (0, pair + 1)
    return (lane >= first + low) & (lane < first + high)


def second_pack_kernel(coarse_ref, y_near_ref, y_far_ref, x_near_ref, x_far_ref):
    x_odd, y_odd = parity("gx"), parity("gy")
    lane = lanes()
    for ref, bottom in ((x_near_ref, 1 - x_odd), (x_far_ref, x_odd)):
        first = bottom * (CROWS - HROWS)
        for i in range(HROWS):
            for c in range(2):
                ref[2 * i + c] = coarse_ref[first + i, c]
        for f in range(3):
            packed = [None] * CREGS
            for away in range(REACH - 1):
                slot, t = divmod(away, EDGE)
                register = t + bottom * (EDGE - 1 - 2 * t)
                source = REACH * (slot + bottom * (5 - 2 * slot))
                for right in range(2):
                    target, start, offset = corner_slot(away, right)
                    take_far = y_odd if right else 1 - y_odd
                    near = y_near_ref[f, register]
                    far = y_far_ref[f, register]
                    halo = jnp.where(jnp.full_like(lane, take_far) == 1, far, near)
                    moved = roll(halo, lax.rem(start + offset - source + 3 * COLS, COLS))
                    if packed[target] is None:
                        packed[target] = moved
                    else:
                        inside = corner_lanes(away, right, lane)
                        packed[target] = jnp.where(inside, moved, packed[target])
            for target in range(CREGS):
                ref[2 * HROWS + CREGS * f + target] = packed[target]


def rim_of(main, left, right, lane):
    own = jnp.where(lane < RIGHT, roll(main, REACH), roll(main, RIGHT - (COLS - 2 * REACH)))
    own = jnp.where(lane < REACH, left, own)
    return jnp.where(lane >= RIM - REACH, right, own)


def products(blocks, table):
    counts = [block.shape[0] * LEVELS for block in blocks]
    values = jnp.concatenate(
        [block.reshape(count, COLS) for block, count in zip(blocks, counts)], axis=0
    )
    high = values.astype(jnp.bfloat16)
    low = (values - high.astype(F32)).astype(jnp.bfloat16)
    result = jnp.dot(
        jnp.concatenate((high, low), axis=1),
        jnp.concatenate((table, table), axis=0),
        preferred_element_type=F32,
    )
    pieces, start = [], 0
    for count in counts:
        pieces.append(result[start : start + count])
        start += count
    return pieces


def stage_products(jobs, table):
    return products([rows[2:-2] for source, _, _, _ in jobs for rows in source], table)


def stage_sums(jobs, across, stage):
    for index, (source, base, background, store) in enumerate(jobs):
        mid = [rows[2:-2] for rows in source]
        count = mid[0].shape[0]
        dy = [across[3 * index + f].reshape(mid[0].shape) for f in range(3)]
        dx = [
            8.0 * (rows[3 : 3 + count] - rows[1 : 1 + count]) - (rows[4:] - rows[:count])
            for rows in source
        ]
        east, north, warm = background
        change = (
            east * dx[0] + north * dy[0] + (dx[1] + dy[2]),
            east * dx[1] + north * dy[1] + warm * dx[0],
            east * dx[2] + north * dy[2] + warm * dy[0],
        )
        for f in range(3):
            moved = mid[f] - change[f]
            if stage == 0:
                moved = (1.0 / 6.0) * moved
            elif stage == 1:
                moved = 0.5 * base[f] + moved
            else:
                moved = (1.0 / 3.0) * base[f] + moved
            store(f, moved)


def refine_columns(values, east_table, north_table, store):
    n = values.shape[0]
    (first,) = products([values[:, 0]], east_table)
    (second,) = products([values[:, 1]], north_table)
    warm = first[:, 2 * COLS :] + second[:, 2 * COLS :]
    for k in range(2):
        cut = slice(COLS * k, COLS * (k + 1))
        for f, result in enumerate((first, second, warm)):
            store(k, f, result[:, cut].reshape(n, LEVELS, COLS))


def merged(f, main, rim, lane):
    value = jnp.where(lane < REACH, roll(rim, -REACH), main)
    value = jnp.where(lane >= COLS - REACH, roll(rim, COLS - 2 * REACH - RIGHT), value)
    return value * scale if f == 0 else value


def inner_kernel(
    coarse_ref, tile_ref, y_near_ref, y_far_ref, edges_ref, inside_ref, refined_ref,
    background, state, first, second, rim_ref,
):
    y_odd = parity("gy")
    lane = lanes()
    east_table, north_table, table = refine_table(0), refine_table(1), difference_table()

    for start in range(0, CROWS, CHUNK):

        def keep(k, f, values, start=start):
            refined_ref[k, f, start : start + CHUNK] = values

        refine_columns(coarse_ref[start : start + CHUNK], east_table, north_table, keep)
    for k in range(2):
        for f in range(3):
            refine_rows(refined_ref, k, f, 0, CROWS, background, 0)

    take_near = (lane >= RIGHT).astype(jnp.int32) == 1 - y_odd
    for row, count, register, slot in slots():
        near_shift = lax.rem((1 - y_odd) * (RIM - REACH) - REACH * slot + COLS, COLS)
        far_shift = lax.rem(y_odd * (RIM - REACH) - REACH * slot + COLS, COLS)
        for f in range(3):
            near = roll(y_near_ref[f, register : register + count], near_shift)
            far = roll(y_far_ref[f, register : register + count], far_shift)
            halo = jnp.where(take_near, near, far)
            rim_ref[f, row : row + count] = rim_of(tile_ref[f, row : row + count], halo, halo, lane)

    class Start:
        def __getitem__(self, index):
            c, f, rows = index
            return (rim_ref if c else tile_ref)[f, rows]

    start_state = Start()
    for s in range(STAGES):
        origin = start_state if s < 3 else state
        buffers = (origin, first, second, state)
        source, target = buffers[s % 3], buffers[s % 3 + 1]
        for c in range(2):
            for f in range(3):
                edges_ref[s, c, f, :HAND] = source[c, f, 2 * s : 2 * s + HAND]
                edges_ref[s, c, f, HAND:] = source[c, f, ROWS - 2 * s - HAND : ROWS - 2 * s]
        low, top = 2 * (s + 1), ROWS - 2 * (s + 1)
        for start in range(low, top, CHUNK):
            stop = min(start + CHUNK, top)
            jobs = []
            for c in range(2):

                def store(f, values, c=c):
                    target[c, f, start:stop] = values

                jobs.append((
                    [source[c, f, start - 2 : stop + 2] for f in range(3)],
                    [origin[c, f, start:stop] for f in range(3)],
                    [background[c, f, start:stop] for f in range(3)],
                    store,
                ))
            stage_sums(jobs, stage_products(jobs, table), s % 3)
    for f in range(3):
        rows = slice(REACH, ROWS - REACH)
        inside_ref[f] = merged(f, state[0, f, rows], state[1, f, rows], lane)


def refine_rows(refined, k, f, start, count, background, first):
    block = refined[k, f, start : start + count]
    factor = scale * scale if f == 2 else scale
    centre = (0.75 * factor) * block
    side = (0.25 * factor) * block
    odd = centre[:-1] + side[1:]
    even = centre[1:] + side[:-1]
    for i in range(count - 1):
        background[k, f, first + 2 * i + 1] = odd[i]
        background[k, f, first + 2 * i + 2] = even[i]


def outer_end(
    side, main_ref, message_ref, edges_ref, refined_ref, refined, background, state, first, second
):
    lane = lanes()
    east_table, north_table, table = refine_table(0), refine_table(1), difference_table()
    own = MARGIN + HROWS
    for k in range(2):
        for f in range(3):
            refined[k, f, pl.ds((1 - side) * HROWS, MARGIN)] = refined_ref[
                k, f, pl.ds(side * (CROWS - MARGIN), MARGIN)
            ]

    def keep(k, f, values):
        refined[k, f, pl.ds(side * MARGIN, HROWS)] = values[:HROWS]

    values = message_ref[: 2 * HROWS + 2].reshape(HROWS + 1, 2, LEVELS, COLS)
    refine_columns(values, east_table, north_table, keep)
    for k in range(2):
        for f in range(3):
            refine_rows(refined, k, f, 0, own, background, 0)

    halo = side * (REACH + HAND)
    for f in range(3):
        state[0, f, pl.ds(halo, REACH)] = main_ref[f]
        for away in range(REACH):
            row = REACH - 1 - away + side * (2 * away - REACH + 1)
            sides = []
            for right in range(2):
                register, start, offset = corner_slot(min(away, REACH - 2), right)
                corner = message_ref[2 * HROWS + CREGS * f + register]
                sides.append(roll(corner, (RIM - REACH) * right - start - offset))
            state[1, f, halo + row] = rim_of(main_ref[f, row], sides[0], sides[1], lane)

    buffers = (state, first, second, state)

    def job_of(c, s):
        source, target = buffers[s % 3], buffers[s % 3 + 1]
        low = 2 * (s + 1) + side * (REACH + 2 - 4 * s)
        handed = REACH + 2 * s - side * 4 * s
        for f in range(3):
            source[c, f, pl.ds(handed, HAND)] = edges_ref[s, c, f, pl.ds(side * HAND, HAND)]

        def store(f, values):
            target[c, f, pl.ds(low, REACH)] = values

        return (
            [source[c, f, pl.ds(low - 2, REACH + 4)] for f in range(3)],
            [state[c, f, pl.ds(low, REACH)] for f in range(3)],
            [background[c, f, pl.ds(low - 4 * side, REACH)] for f in range(3)],
            store,
        )

    waiting = [None, None]
    for s in range(STAGES + 1):
        for c in range(2):
            if waiting[c] is not None:
                stage_sums(waiting[c][0], waiting[c][1], (s - 1) % 3)
            if s < STAGES:
                jobs = [job_of(c, s)]
                waiting[c] = (jobs, stage_products(jobs, table))
    rows = pl.ds(REACH - 2 * HAND * side, REACH)
    return [merged(f, state[0, f, rows], state[1, f, rows], lane) for f in range(3)]


def place(out_ref, f, row, value):
    rows = out_ref.shape[0] // (3 * LEVELS)
    out_ref[pl.ds(f * LEVELS * rows + row, LEVELS, stride=rows), :] = value


def near_end_kernel(
    main_ref, message_ref, edges_ref, refined_ref, inside_ref, end_ref,
    refined, background, state, first, second, out_ref, sem,
):
    side = 1 - parity("gx")
    for f in range(3):
        for row in range(ROWS - 2 * REACH):
            place(out_ref, f, REACH + row, inside_ref[f, row])
    ends = outer_end(
        side, main_ref, message_ref, edges_ref, refined_ref, refined, background, state, first, second
    )
    for f in range(3):
        for row in range(REACH):
            place(out_ref, f, row + side * (ROWS - REACH), ends[f][row])
    source = out_ref.reshape(3 * LEVELS, ROWS, COLS)
    rows = pl.ds(pl.multiple_of(side * OWN, 8), ROWS - OWN)
    copy = pltpu.make_async_copy(source.at[:, rows], end_ref.at[:, rows], sem.at[0])
    copy.start()
    copy.wait()


def far_end_kernel(
    main_ref, message_ref, edges_ref, refined_ref, inside_ref, before_ref, end_ref,
    refined, background, state, first, second, out_ref, sems,
):
    del before_ref
    side = parity("gx")
    spare = OWN - REACH
    for f in range(3):
        for row in range(spare):
            inner = row + side * (ROWS - 2 * REACH - spare)
            place(out_ref, f, row + (1 - side) * REACH, inside_ref[f, inner])
    ends = outer_end(
        side, main_ref, message_ref, edges_ref, refined_ref, refined, background, state, first, second
    )
    target = out_ref.reshape(3 * LEVELS, OWN, COLS)
    rows = pl.ds(pl.multiple_of(side * (ROWS - OWN), 8), OWN)
    copies = []
    for f in range(3):
        for row in range(REACH):
            place(out_ref, f, row + side * spare, ends[f][row])
        field = pl.ds(f * LEVELS, LEVELS)
        copies.append(
            pltpu.make_async_copy(target.at[field], end_ref.at[field, rows], sems.at[f])
        )
        copies[f].start()
    for copy in copies:
        copy.wait()


def refine_table(north):
    row = lax.broadcasted_iota(jnp.int32, (COLS, 2 * COLS), 0)
    lane = lax.broadcasted_iota(jnp.int32, (COLS, 2 * COLS), 1)
    rim = lane - COLS
    column = jnp.where(rim < RIGHT, rim - REACH, rim - RIGHT + COLS - 2 * REACH)
    column = jnp.where(lane < COLS, lane, column)
    centre = lax.shift_right_arithmetic(column, 1) + MARGIN
    side = centre - 1 + 2 * (column & 1)

    def weights(window, used):
        weight = jnp.where(window == centre, 0.75, jnp.where(window == side, 0.25, 0.0))
        return jnp.where(used & (rim < RIM), weight, 0.0).astype(jnp.bfloat16)

    wind = weights(row, row < WINDOW)
    warm = weights(row - WINDOW + HALF * north, (row >= WINDOW) & (row < WINDOW + HALF))
    return jnp.concatenate((wind, warm), axis=1)


def difference_table():
    source = lax.broadcasted_iota(jnp.int32, (COLS, COLS), 0)
    lane = lax.broadcasted_iota(jnp.int32, (COLS, COLS), 1)
    ahead = (source - lane) & (COLS - 1)
    table = jnp.where(ahead == 1, 8.0, 0.0) - jnp.where(ahead == COLS - 1, 8.0, 0.0)
    table = table - jnp.where(ahead == 2, 1.0, 0.0) + jnp.where(ahead == COLS - 2, 1.0, 0.0)
    return table.astype(jnp.bfloat16)


def call(
    kernel, outputs, scratch=(), limit=48, microseconds=1, fetched=(), sent=False, semaphores=0,
    aliases=None,
):
    here, there = pl.BlockSpec(memory_space=pltpu.VMEM), pl.BlockSpec(memory_space=pltpu.HBM)

    def run(*operands):
        return pl.pallas_call(
            kernel,
            out_shape=[jax.ShapeDtypeStruct(shape, F32) for shape in outputs],
            in_specs=[there if i in fetched else here for i in range(len(operands))],
            out_specs=[there if sent else here] * len(outputs),
            scratch_shapes=[pltpu.VMEM(shape, F32) for shape in scratch]
            + ([pltpu.SemaphoreType.DMA((semaphores,))] if semaphores else []),
            input_output_aliases=aliases or {},
            compiler_params=pltpu.CompilerParams(vmem_limit_bytes=limit * 2**20),
            cost_estimate=pl.CostEstimate(
                flops=0, bytes_accessed=3_000_000 * microseconds, transcendentals=0
            ),
        )(*operands)

    return run


def local(les_wind, les_temp, acoustic_start):
    block = (LEVELS, COLS)
    groups = lax.axis_size("gy")
    (packed,) = call(
        strip_kernel,
        [(groups, 2, 2) + block],
        scratch=[les_wind.shape, les_temp.shape, (groups, 2, 2) + block],
        fetched=(0, 1),
        sent=True,
        semaphores=4,
        limit=PACK_LIMIT,
    )(les_wind, les_temp)
    tile, x_near, x_far, y_near, y_far = call(
        tile_kernel, [(3, ROWS) + block] + 2 * [(3, REACH) + block] + 2 * [(3, SIDE) + block]
    )(acoustic_start.reshape(3 * LEVELS * ROWS, COLS))
    coarse = lax.all_to_all(packed, "gy", split_axis=0, concat_axis=0, tiled=True)
    coarse = coarse.reshape((CROWS, 2) + block)
    x_near, x_far = swap_near(x_near, "gx"), swap_far(x_far, "gx")
    y_near, y_far = swap_near(y_near, "gy"), swap_far(y_far, "gy")
    s_near, s_far = call(second_pack_kernel, 2 * [(2 * HROWS + 3 * CREGS,) + block])(
        coarse, y_near, y_far
    )
    s_near, s_far = swap_near(s_near, "gx"), swap_far(s_far, "gx")
    edges, inside, refined = call(
        inner_kernel,
        [(STAGES, 2, 3, 2 * HAND) + block, (3, ROWS - 2 * REACH) + block, (2, 3, CROWS) + block],
        scratch=4 * [(2, 3, ROWS) + block] + [(3, ROWS) + block],
        microseconds=6,
    )(coarse, tile, y_near, y_far)
    scratch = [(2, 3, MARGIN + HROWS) + block, (2, 3, 2 * (MARGIN + HROWS)) + block]
    scratch += 3 * [(2, 3, REACH + REACH + HAND) + block]
    whole = (3 * LEVELS, ROWS, COLS)
    (near,) = call(
        near_end_kernel,
        [whole],
        scratch=scratch + [(3 * LEVELS * ROWS, COLS)],
        microseconds=3,
        sent=True,
        semaphores=1,
    )(x_near, s_near, edges, refined, inside)
    (end,) = call(
        far_end_kernel,
        [whole],
        scratch=scratch + [(3 * LEVELS * OWN, COLS)],
        microseconds=3,
        fetched=(5,),
        sent=True,
        semaphores=3,
        aliases={5: 0},
    )(x_far, s_far, edges, refined, inside, near)
    return end.reshape(acoustic_start.shape)


def solution(mesh):
    in_specs = (
        P(None, None, ("gx", "gy"), None),
        P(None, ("gx", "gy"), None),
        P(None, None, "gx", "gy"),
    )
    out_specs = P(None, None, "gx", "gy")
    return jax.shard_map(local, mesh=mesh, in_specs=in_specs, out_specs=out_specs, check_vma=False)
```
